128 devices in a mesh: db: 16 (over z, y_lo, core), mp: 8 (over x, y_hi).
Axes of the slice: x: 4, y: 4 (y_hi: 2, y_lo: 2; y = y_hi * 2 + y_lo), z: 4, core: 2. Of those that a mesh axis runs over, the one named last changes fastest.
Arguments:
- queries: bfloat16 [4096, 4096], P('db', 'mp'), may hold values from -80 to 80
- database: bfloat16 [256, 128, 8192], P('db', None, 'mp'), may hold values from -6 to 6
- neighbor_owner: int32 [64, 2], P('db'), may hold values from 0 to 15, all different within a row; in each aligned block of 4 rows (0 to 3, 4 to 7, ...) at most 2 rows name the same one
- neighbor_slot: int32 [64, 2], P('db'), may hold values from 0 to 15
- key_weight: bfloat16 [8192, 4096], P(None, 'mp'), may hold values from -0.0625 to 0.0625
- value_weight: bfloat16 [8192, 4096], P(None, 'mp'), may hold values from -0.0625 to 0.0625
- cotangent: bfloat16 [4096, 4096], P('db', 'mp'), may hold values from -8 to 8
Outputs:
- attended: bfloat16 [4096, 4096], P('db', 'mp')
- query_grad: bfloat16 [4096, 4096], P('db', 'mp')
- value_weight_grad: float32 [8192, 4096], P('db', 'mp')
The draws below stay inside these ranges and needn't reach their ends.
Inputs may be any that keep to these rules, and one draw needn't show every extreme that they name: `neighbor_owner`: the 2 owners of one query span differ. Among the 4 query spans of one index of db, no owner is named more than 2 times, and in some such block one owner is named exactly 2 times.
All inputs are finite; a program needn't handle non-finite values.
Results may differ from the reference program's by a relative error of at most 0.023.
The reference program's roundings to bfloat16 on the way count: a program that leaves them out, or rounds other values in their place, can miss the bound.
Values may be sent and summed in bfloat16 or wider, within the bound.
No kernel may reach another device: no remote copies, remote signals or barrier semaphores. Data moves between devices by JAX's collectives and lax.ppermute only.
A program may use at most 128 MiB of HBM per device.

```python
import math
import jax
import jax.numpy as jnp
import numpy as np
from jax import lax

D = 8192
HEAD_DIM = 128
NUM_HEADS = 32
SPAN_LEN = 64
NEIGHBORS = 2
NEIGHBOR_LEN = 128
CAPACITY = 2
CH_DEV = 4
DB_DEV = 16
SPANS = 64
TOKENS = 4096
DB_SPANS = 256
N_DB = 16


def draw_queries(key, part):
    key = jax.random.fold_in(key, 5)
    entries = 2.0 * jax.random.normal(key, (TOKENS, NUM_HEADS * HEAD_DIM), jnp.float32)
    return jnp.clip(entries, -8.0, 8.0).astype(jnp.bfloat16)


def set_ends(drawn, own_key, least, largest):
    shape = drawn.shape
    spot = [jax.random.randint(jax.random.fold_in(own_key, axis), (), 0, shape[axis]) for axis in range(len(shape))]
    drawn = drawn.at[tuple(spot)].set(least)
    longest = shape.index(max(shape))
    spot[longest] = (spot[longest] + 1) % shape[longest]
    return drawn.at[tuple(spot)].set(largest)


def shard_levels(rng, dims, cuts, least, largest):
    level = 1.0
    for axis_at, shards_of in cuts:
        steps = jax.random.uniform(jax.random.fold_in(jax.random.fold_in(rng, 6), axis_at), (shards_of,), jnp.float32, least / len(cuts), largest / len(cuts))
        level = level * jnp.repeat(jnp.exp(steps), dims[axis_at] // shards_of).reshape((-1,) + (1,) * (len(dims) - 1 - axis_at))
    return level


def shared_out(rng, own, number, rows, amount, top, bound, slope):
    ranking = jax.random.permutation(rng, amount)
    crowded, ordinary = portions_of(amount, rows * top, bound, slope, True), portions_of(amount, rows * top, bound, slope, False)
    places = jnp.arange(amount)

    def named(sizes, rotation):
        used = int((sizes > 0).sum())
        fixed = max(1, used // 4)
        passed = fixed + (places - fixed + rotation * (used - fixed)) % max(1, amount - fixed)
        return jnp.zeros((amount,), jnp.int32).at[ranking[jnp.where(places < fixed, places, passed)]].set(jnp.asarray(sizes, jnp.int32))

    sizes = jnp.where(number % 4 == 0, named(crowded, number // 4), named(ordinary, number - number // 4 - 1))
    mixed = jax.random.permutation(jax.random.fold_in(own, 3), amount)
    donor, taker = mixed[0:amount // 2 * 2:2], mixed[1:amount // 2 * 2:2]
    slack = jnp.minimum(sizes[donor] - 1, bound - sizes[taker]) // 2
    slack = jnp.where((donor == ranking[0]) | (taker == ranking[0]) | (sizes[taker] == 0), 0, jnp.maximum(slack, 0))
    passed = jax.random.randint(jax.random.fold_in(own, 4), (amount // 2,), 0, 1 << 20) % (slack + 1)
    sizes = sizes.at[donor].add(-passed).at[taker].add(passed)
    labels = jnp.searchsorted(jnp.cumsum(sizes), jnp.arange(rows * top), side="right").astype(jnp.int32)
    table = labels.reshape(top, rows).T
    table = table[jax.random.permutation(jax.random.fold_in(own, 1), rows)]
    rotation = jax.random.randint(jax.random.fold_in(own, 2), (rows, 1), 0, top)
    return jnp.take_along_axis(table, (jnp.arange(top)[None, :] + rotation) % top, axis=1)


def portions_of(number_of, total, reach, lean, full):
    loads = [(1 << 20) // math.isqrt(standing ** lean) + 1 for standing in range(1, number_of + 1)]
    largest = reach if full else min(reach, max(-(-total // number_of), total * loads[0] // sum(loads)))
    least = 1 if total - largest >= number_of - 1 else 0
    given, surplus = [largest] + [least] * (number_of - 1), total - largest - least * (number_of - 1)
    while surplus > 0:
        free = [i for i in range(1, number_of) if given[i] < largest] or [i for i in range(1, number_of) if given[i] < reach]
        whole, budget = sum([loads[i] for i in free]), surplus
        for i in free:
            addition = min(reach - given[i], max(1, budget * loads[i] // whole), surplus)
            given[i] = given[i] + addition
            surplus = surplus - addition
    return np.array(given)


def centred(rng, extent, deviation, limit, cuts=(), dtype=jnp.bfloat16):
    drawn = deviation * jax.random.normal(rng, extent, jnp.float32)
    if cuts:
        drawn = drawn * shard_levels(rng, extent, cuts, -0.22, 0.18)
    return jnp.clip(drawn, -limit, limit).astype(dtype)


def setup_inputs(seed: int = 0) -> dict:
    arg_keys = jax.random.split(jax.random.key(seed), 8)
    queries = draw_queries(jax.random.fold_in(arg_keys[7], 71), 0)
    database = centred(arg_keys[1], (DB_SPANS, NEIGHBOR_LEN, D), 1.0, 6.0, ((0, 16), (2, 8)))
    neighbor_owner_keys = jax.random.split(jax.random.fold_in(arg_keys[2], 1), SPANS // CH_DEV)
    neighbor_owner_turns = jax.random.permutation(jax.random.fold_in(arg_keys[2], 3), SPANS // CH_DEV)
    neighbor_owner = jax.vmap(lambda own, number: shared_out(jax.random.fold_in(arg_keys[2], 2), own, number, CH_DEV, N_DB, NEIGHBORS, CAPACITY, 2))(neighbor_owner_keys, neighbor_owner_turns).reshape((SPANS, NEIGHBORS))
    neighbor_slot = set_ends(jax.random.randint(arg_keys[3], (SPANS, NEIGHBORS), 0, DB_DEV), jax.random.fold_in(arg_keys[3], 1), 0, DB_DEV - 1).astype(jnp.int32)
    key_weight = centred(arg_keys[4], (D, NUM_HEADS * HEAD_DIM), D ** -0.5, 0.0625, ((1, 8),))
    value_weight = centred(arg_keys[5], (D, NUM_HEADS * HEAD_DIM), D ** -0.5, 0.0625, ((1, 8),))
    cotangent = centred(arg_keys[6], (TOKENS, NUM_HEADS * HEAD_DIM), 2.0, 8.0, ((0, 16), (1, 8)))
    return {"queries": queries, "database": database, "neighbor_owner": neighbor_owner, "neighbor_slot": neighbor_slot, "key_weight": key_weight, "value_weight": value_weight, "cotangent": cotangent}


def span_attention(query_blocks, key_blocks, value_blocks, grad_blocks, score_scale):
    query_full = query_blocks.astype(jnp.float32)
    key_full = key_blocks.astype(jnp.float32)
    value_full = value_blocks.astype(jnp.float32)
    grad_full = grad_blocks.astype(jnp.float32)
    scores = jnp.einsum("cqhd,ckhd->chqk", query_full, key_full) * score_scale
    highest = jnp.max(scores, axis=-1, keepdims=True)
    raised = jnp.exp(scores - highest)
    probabilities = raised / jnp.sum(raised, axis=-1, keepdims=True)
    weights = probabilities.astype(jnp.bfloat16).astype(jnp.float32)
    attended = jnp.einsum("chqk,ckhd->cqhd", weights, value_full).astype(jnp.bfloat16)
    value_grad = jnp.einsum("chqk,cqhd->ckhd", weights, grad_full).astype(jnp.bfloat16)
    prob_grad = jnp.einsum("cqhd,ckhd->chqk", grad_full, value_full)
    centre = jnp.sum(probabilities * prob_grad, axis=-1, keepdims=True)
    score_grad = (probabilities * (prob_grad - centre)).astype(jnp.bfloat16).astype(jnp.float32)
    query_grad = (jnp.einsum("chqk,ckhd->cqhd", score_grad, key_full) * score_scale).astype(jnp.bfloat16)
    return attended, query_grad, value_grad


def reference(queries, database, neighbor_owner, neighbor_slot, key_weight, value_weight, cotangent):
    score_scale = HEAD_DIM ** -0.5
    full_width = key_weight.shape[1]
    head_count = full_width // HEAD_DIM
    model_width = database.shape[2]
    span_ids = (neighbor_owner * DB_DEV + neighbor_slot).astype(jnp.int32)
    group_ids = span_ids.reshape(N_DB, CH_DEV * NEIGHBORS)
    group_queries = queries.reshape(N_DB, CH_DEV, SPAN_LEN, head_count, HEAD_DIM)
    group_grads = cotangent.reshape(N_DB, CH_DEV, SPAN_LEN, head_count, HEAD_DIM)

    def group_step(total, inputs):
        picked, query_blocks, grad_blocks = inputs
        encoded_rows = jnp.take(database, picked, axis=0).reshape(-1, model_width)
        key_rows = jnp.dot(encoded_rows, key_weight, preferred_element_type=jnp.float32).astype(jnp.bfloat16)
        value_rows = jnp.dot(encoded_rows, value_weight, preferred_element_type=jnp.float32).astype(jnp.bfloat16)
        key_blocks = key_rows.reshape(CH_DEV, NEIGHBORS * NEIGHBOR_LEN, head_count, HEAD_DIM)
        value_blocks = value_rows.reshape(CH_DEV, NEIGHBORS * NEIGHBOR_LEN, head_count, HEAD_DIM)
        attended, query_grad, value_grad = span_attention(query_blocks, key_blocks, value_blocks, grad_blocks, score_scale)
        value_part = jnp.dot(encoded_rows.T, value_grad.reshape(-1, full_width), preferred_element_type=jnp.float32).astype(jnp.bfloat16)
        value_part = lax.optimization_barrier(value_part)
        return total + value_part.astype(jnp.float32), (attended, query_grad)

    empty_sum = jnp.zeros((model_width, full_width), jnp.float32)
    value_total, (attended, query_grad) = lax.scan(group_step, empty_sum, (group_ids, group_queries, group_grads))
    return attended.reshape(-1, full_width), query_grad.reshape(-1, full_width), value_total
```

```python
import functools

import jax
import jax.numpy as jnp
from jax import lax
from jax.experimental import pallas as pl
from jax.experimental.pallas import tpu as pltpu
from jax.sharding import Mesh
from jax.sharding import PartitionSpec as P

HEAD_DIM = 128
SPAN_LEN = 64
CHUNKS = (32, 32, 32, 32)
DB = ("z", "ylo", "core")
MP = ("x", "yhi")
VMEM_LIMIT = 40 * 1024 * 1024
TARGETS = ((2, 1), (2, 0), (1, 1), (3, 1), (1, 0), (3, 0), (0, 1), (0, 0))


def ring(values, axis, shift, size):
    return lax.ppermute(values, axis, [(i, (i + shift) % size) for i in range(size)])


def pack_kernel(first, rows, place, wanted, own, beside, across, corner, packet, sems):
    z, ylo, core = place[0], place[1], place[2]
    count = packet.shape[0]
    pools = (own, beside, across, corner)
    cuts = (first, 0, first, 0)

    def each(act):
        for i in range(count):
            owner = wanted[0, i]
            slot = wanted[0, count + i]
            here = owner // 4 == z
            which = (owner // 2 % 2 + ylo) % 2 + 2 * ((owner % 2 + core) % 2)
            for n, (pool, cut) in enumerate(zip(pools, cuts)):
                @pl.when(here & (which == n))
                def _():
                    act(
                        pltpu.make_async_copy(
                            pool.at[slot, pl.ds(cut, rows)], packet.at[i], sems.at[i]
                        )
                    )

    each(lambda copy: copy.start())
    each(lambda copy: copy.wait())


def merge_kernel(first, rows, place, wanted, own, beside, across, corner, one, two, three, merged, sems):
    z, ylo, core = place[0], place[1], place[2]
    count = merged.shape[0]
    pools = (own, beside, across, corner)
    cuts = (first, 0, first, 0)

    def each(act):
        for i in range(count):
            owner = wanted[0, i]
            slot = wanted[0, count + i]
            away = (owner // 4 + 4 - z) % 4
            which = (owner // 2 % 2 + ylo) % 2 + 2 * ((owner % 2 + core) % 2)
            for n, (pool, cut) in enumerate(zip(pools, cuts)):
                @pl.when((away == 0) & (which == n))
                def _():
                    act(
                        pltpu.make_async_copy(
                            pool.at[slot, pl.ds(cut, rows)], merged.at[i], sems.at[i]
                        )
                    )
            for n, packet in enumerate((one, two, three)):
                @pl.when(away == n + 1)
                def _():
                    act(pltpu.make_async_copy(packet.at[i], merged.at[i], sems.at[i]))

    each(lambda copy: copy.start())
    each(lambda copy: copy.wait())


def copies_call(kernel, name, count, rows, width, place, wanted, arrays):
    return pl.pallas_call(
        kernel,
        name=name,
        out_shape=jax.ShapeDtypeStruct((count, rows, width), jnp.bfloat16),
        grid_spec=pltpu.PrefetchScalarGridSpec(
            num_scalar_prefetch=2,
            grid=(1,),
            in_specs=[pl.BlockSpec(memory_space=pl.ANY)] * len(arrays),
            out_specs=pl.BlockSpec(memory_space=pl.ANY),
            scratch_shapes=[pltpu.SemaphoreType.DMA((count,))],
        ),
        cost_estimate=pl.CostEstimate(
            flops=0, bytes_accessed=2 * count * rows * width * 2, transcendentals=0
        ),
    )(place, wanted, *arrays)


def project_kernel(
    place, own, left, right, far0, far1, key_weight, value_weight, keys, values, encoded, key_sum, value_sum
):
    step = pl.program_id(0)

    @pl.when(step == 0)
    def _():
        key_sum[...] = jnp.zeros_like(key_sum)
        value_sum[...] = jnp.zeros_like(value_sum)

    def add(piece):
        rows = piece[0]
        encoded[0] = rows
        key_sum[...] += jnp.dot(rows, key_weight[...], preferred_element_type=jnp.float32)
        value_sum[...] += jnp.dot(rows, value_weight[...], preferred_element_type=jnp.float32)

    for piece, (low, high) in (
        (own, (0, 2)), (left, (2, 4)), (right, (4, 6)), (far0, (6, 7)), (far1, (7, 8))
    ):
        pl.when((step >= low) & (step < high))(functools.partial(add, piece))

    @pl.when(step == 7)
    def _():
        keys[...] = key_sum[...].astype(keys.dtype)
        values[...] = value_sum[...].astype(values.dtype)


def project(place, pieces, key_weight, value_weight):
    own, left, right, far0, far1 = pieces
    rows, depth = own.shape[1], own.shape[2]
    width = key_weight.shape[1]

    def slice_of(step, place):
        hop = step // 2
        shift = jnp.where(hop == 0, 0, jnp.where(hop == 1, 3, jnp.where(hop == 2, 1, 2)))
        return (place[3] + shift) % 4 * 2 + step % 2

    def pair(low):
        return pl.BlockSpec(
            (1, rows, depth), lambda step, place: (jnp.clip(step - low, 0, 1), 0, 0)
        )

    single = pl.BlockSpec((1, rows, depth), lambda step, place: (0, 0, 0))
    weight = pl.BlockSpec((depth, width), lambda step, place: (slice_of(step, place), 0))
    whole = pl.BlockSpec((rows, width), lambda step, place: (0, 0))
    return pl.pallas_call(
        project_kernel,
        name="project",
        out_shape=(
            jax.ShapeDtypeStruct((rows, width), jnp.bfloat16),
            jax.ShapeDtypeStruct((rows, width), jnp.bfloat16),
            jax.ShapeDtypeStruct((8, rows, depth), jnp.bfloat16),
        ),
        grid_spec=pltpu.PrefetchScalarGridSpec(
            num_scalar_prefetch=1,
            grid=(8,),
            in_specs=[pair(0), pair(2), pair(4), single, single, weight, weight],
            out_specs=(
                whole,
                whole,
                pl.BlockSpec((1, rows, depth), lambda step, place: (slice_of(step, place), 0, 0)),
            ),
            scratch_shapes=[pltpu.VMEM((rows, width), jnp.float32)] * 2,
        ),
        compiler_params=pltpu.CompilerParams(vmem_limit_bytes=VMEM_LIMIT),
        cost_estimate=pl.CostEstimate(
            flops=4 * rows * 8 * depth * width,
            bytes_accessed=32 * depth * width + 32 * rows * depth,
            transcendentals=0,
        ),
    )(place, own, left, right, far0, far1, key_weight, value_weight)


def span_rows(parts, span, low, high):
    pieces = []
    for part in parts:
        size = part.shape[0] // 4
        pieces.append(part[span * size:(span + 1) * size, low:high])
    return jnp.concatenate(pieces, axis=0)


def weigh_kernel(chunks, *refs):
    queries, cotangent = refs[0], refs[1]
    key_parts = refs[2:2 + chunks]
    chances, gradient, stacked = refs[2 + chunks:]
    width = queries.shape[1]
    scale = HEAD_DIM ** (-0.5)
    for span in range(4):
        tokens = slice(span * SPAN_LEN, (span + 1) * SPAN_LEN)
        for head in range(width // HEAD_DIM):
            low, high = head * HEAD_DIM, (head + 1) * HEAD_DIM
            keys = span_rows(key_parts, span, low, high)
            scores = lax.dot_general(
                queries[tokens, low:high], keys, (((1,), (1,)), ((), ())),
                preferred_element_type=jnp.float32,
            ) * scale
            raised = jnp.exp(scores - jnp.max(scores, axis=-1, keepdims=True))
            found = raised / jnp.sum(raised, axis=-1, keepdims=True)
            chances[span * (width // HEAD_DIM) + head] = found
            part = lax.dot_general(
                found.astype(jnp.bfloat16), cotangent[tokens, low:high], (((0,), (0,)), ((), ())),
                preferred_element_type=jnp.float32,
            ).astype(jnp.bfloat16)
            base, start = 0, 0
            for key_part in key_parts:
                size = key_part.shape[0] // 4
                at = base + span * size
                stacked[at:at + size, low:high] = part[start:start + size]
                start += size
                base += key_part.shape[0]
    gradient[...] = stacked[...].T


def weigh(queries, cotangent, key_parts):
    tokens, width = queries.shape
    rows = sum(part.shape[0] for part in key_parts)
    heads = width // HEAD_DIM
    vmem = pl.BlockSpec(memory_space=pltpu.VMEM)
    return pl.pallas_call(
        functools.partial(weigh_kernel, len(key_parts)),
        name="weigh",
        out_shape=(
            jax.ShapeDtypeStruct((4 * heads, SPAN_LEN, rows // 4), jnp.float32),
            jax.ShapeDtypeStruct((width, rows), jnp.bfloat16),
        ),
        in_specs=[vmem] * (2 + len(key_parts)),
        out_specs=(vmem, vmem),
        scratch_shapes=[pltpu.VMEM((rows, width), jnp.bfloat16)],
        compiler_params=pltpu.CompilerParams(vmem_limit_bytes=VMEM_LIMIT),
        cost_estimate=pl.CostEstimate(
            flops=4 * tokens * (rows // 4) * width,
            bytes_accessed=8 * rows * width,
            transcendentals=tokens * rows,
        ),
    )(queries, cotangent, *key_parts)


def attend_kernel(chunks, *refs):
    cotangent, chances = refs[0], refs[1]
    key_parts = refs[2:2 + chunks]
    value_parts = refs[2 + chunks:2 + 2 * chunks]
    attended, query_grad = refs[2 + 2 * chunks:]
    width = cotangent.shape[1]
    scale = HEAD_DIM ** (-0.5)
    for span in range(4):
        tokens = slice(span * SPAN_LEN, (span + 1) * SPAN_LEN)
        for head in range(width // HEAD_DIM):
            low, high = head * HEAD_DIM, (head + 1) * HEAD_DIM
            keys = span_rows(key_parts, span, low, high)
            values = span_rows(value_parts, span, low, high)
            found = chances[span * (width // HEAD_DIM) + head]
            attended[tokens, low:high] = jnp.dot(
                found.astype(jnp.bfloat16), values, preferred_element_type=jnp.float32
            ).astype(jnp.bfloat16)
            slope = lax.dot_general(
                cotangent[tokens, low:high], values, (((1,), (1,)), ((), ())),
                preferred_element_type=jnp.float32,
            )
            centre = jnp.sum(found * slope, axis=-1, keepdims=True)
            score_grad = (found * (slope - centre)).astype(jnp.bfloat16)
            query_grad[tokens, low:high] = (
                jnp.dot(score_grad, keys, preferred_element_type=jnp.float32) * scale
            ).astype(jnp.bfloat16)


def attend(cotangent, chances, key_parts, value_parts):
    tokens, width = cotangent.shape
    rows = sum(part.shape[0] for part in key_parts)
    vmem = pl.BlockSpec(memory_space=pltpu.VMEM)
    return pl.pallas_call(
        functools.partial(attend_kernel, len(key_parts)),
        name="attend",
        out_shape=(
            jax.ShapeDtypeStruct((tokens, width), jnp.bfloat16),
            jax.ShapeDtypeStruct((tokens, width), jnp.bfloat16),
        ),
        in_specs=[vmem] * (2 + 2 * len(key_parts)),
        out_specs=(vmem, vmem),
        compiler_params=pltpu.CompilerParams(vmem_limit_bytes=VMEM_LIMIT),
        cost_estimate=pl.CostEstimate(
            flops=6 * tokens * (rows // 4) * width,
            bytes_accessed=8 * rows * width,
            transcendentals=0,
        ),
    )(cotangent, chances, *key_parts, *value_parts)


def term_kernel(chunks, adds, *refs):
    gradient = refs[1]
    encoded_parts = refs[2:2 + chunks]
    output = refs[-1]
    total, base = None, 0
    for encoded in encoded_parts:
        rows = encoded.shape[1]
        part = jnp.dot(
            gradient[:, base:base + rows], encoded[0], preferred_element_type=jnp.float32
        )
        total = part if total is None else total + part
        base += rows
    total = total.astype(jnp.bfloat16)
    if adds:
        total = (total.astype(jnp.float32) + refs[2 + chunks][0].astype(jnp.float32)).astype(
            jnp.bfloat16
        )
    output[0] = total


def weight_terms(blocks, gradient, encoded_parts, arrived=None, offset=0):
    count = blocks.shape[0] - 1
    width, rows = gradient.shape
    depth = encoded_parts[0].shape[2] // 2
    in_specs = [pl.BlockSpec((width, rows), lambda n, blocks: (0, 0))]
    for part in encoded_parts:
        in_specs.append(
            pl.BlockSpec(
                (1, part.shape[1], depth), lambda n, blocks: (blocks[n], 0, blocks[count])
            )
        )
    operands = [gradient, *encoded_parts]
    if arrived is not None:
        in_specs.append(pl.BlockSpec((1, width, depth), lambda n, blocks: (offset + n, 0, 0)))
        operands.append(arrived)
    return pl.pallas_call(
        functools.partial(term_kernel, len(encoded_parts), arrived is not None),
        name="terms",
        out_shape=jax.ShapeDtypeStruct((count, width, depth), jnp.bfloat16),
        grid_spec=pltpu.PrefetchScalarGridSpec(
            num_scalar_prefetch=1,
            grid=(count,),
            in_specs=in_specs,
            out_specs=pl.BlockSpec((1, width, depth), lambda n, blocks: (n, 0, 0)),
        ),
        compiler_params=pltpu.CompilerParams(vmem_limit_bytes=VMEM_LIMIT),
        cost_estimate=pl.CostEstimate(
            flops=2 * count * width * rows * depth,
            bytes_accessed=2 * rows * width + 2 * count * depth * (rows + 2 * width),
            transcendentals=0,
        ),
    )(blocks, *operands)


def total_kernel(*refs):
    output = refs[-1]
    total = refs[0][0].astype(jnp.float32)
    for block in refs[1:-1]:
        total += block[0].astype(jnp.float32)
    output[...] = total.T


def add_blocks(blocks):
    width, depth = blocks[0].shape[1:]
    vmem = pl.BlockSpec(memory_space=pltpu.VMEM)
    return pl.pallas_call(
        total_kernel,
        name="total",
        out_shape=jax.ShapeDtypeStruct((depth, width), jnp.float32),
        in_specs=[vmem] * len(blocks),
        out_specs=vmem,
        compiler_params=pltpu.CompilerParams(vmem_limit_bytes=VMEM_LIMIT),
        cost_estimate=pl.CostEstimate(
            flops=len(blocks) * width * depth,
            bytes_accessed=(2 * len(blocks) + 4) * width * depth,
            transcendentals=0,
        ),
    )(*blocks)


def per_device(
    queries, database, neighbor_owner, neighbor_slot, key_weight, value_weight, cotangent
):
    z, ylo, core = lax.axis_index("z"), lax.axis_index("ylo"), lax.axis_index("core")
    x, yhi = lax.axis_index("x"), lax.axis_index("yhi")
    place = jnp.stack([z, ylo, core, x, yhi]).astype(jnp.int32)
    count = neighbor_owner.shape[0] * neighbor_owner.shape[1]
    width = database.shape[2]
    wanted = jnp.concatenate(
        [neighbor_owner.reshape(1, count), neighbor_slot.reshape(1, count)], axis=1
    )
    asked = [wanted] + [ring(wanted, "z", -n, 4) for n in (1, 2, 3)]
    across = ring(database, "core", 1, 2)

    key_parts, value_parts, encoded_parts = [], [], []
    first = 0
    for rows in CHUNKS:
        beside = ring(database[:, first:first + rows], "ylo", 1, 2)
        corner = ring(beside, "core", 1, 2)
        pools = (database, beside, across, corner)
        packets = [
            ring(
                copies_call(
                    functools.partial(pack_kernel, first, rows), "pack", count, rows, width,
                    place, asked[n], pools,
                ),
                "z", n, 4,
            )
            for n in (1, 2, 3)
        ]
        own = copies_call(
            functools.partial(merge_kernel, first, rows), "merge", count, rows, width,
            place, wanted, (*pools, packets[2], packets[1], packets[0]),
        ).reshape(1, count * rows, width)
        other = ring(own, "yhi", 1, 2)
        pair = jnp.where(
            yhi == 0,
            jnp.concatenate([own, other], axis=0),
            jnp.concatenate([other, own], axis=0),
        )
        left = ring(pair, "x", 1, 4)
        right = ring(pair, "x", -1, 4)
        far0 = ring(left[0:1], "x", 1, 4)
        far1 = ring(right[1:2], "x", -1, 4)
        keys, values, encoded = project(
            place, (pair, left, right, far0, far1), key_weight, value_weight
        )
        key_parts.append(keys)
        value_parts.append(values)
        encoded_parts.append(encoded)
        first += rows

    chances, gradient = weigh(queries, cotangent, key_parts)

    order = [(z + dz) % 4 * 2 + (ylo + dy) % 2 for dz, dy in TARGETS]
    sent = []
    for low, high in ((0, 4), (4, 8)):
        blocks = jnp.stack([*order[low:high], 1 - core]).astype(jnp.int32)
        terms = weight_terms(blocks, gradient, encoded_parts)
        sent.append(ring(terms, "core", 1, 2))
    totals = []
    for n, (dz, dy) in enumerate(TARGETS):
        blocks = jnp.stack([order[n], core]).astype(jnp.int32)
        block = weight_terms(blocks, gradient, encoded_parts, sent[n // 4], n % 4)
        if (dz, dy) != (0, 0):
            block = lax.ppermute(
                block, ("z", "ylo"),
                [
                    (a * 2 + b, (a + dz) % 4 * 2 + (b + dy) % 2)
                    for a in range(4) for b in range(2)
                ],
            )
        totals.append(block)
    value_weight_grad = add_blocks(totals)
    attended, query_grad = attend(cotangent, chances, key_parts, value_parts)
    return attended, query_grad, value_weight_grad


def solution(mesh):
    inner = Mesh(mesh.devices.reshape(4, 2, 2, 4, 2), (*DB, *MP))
    return jax.shard_map(
        per_device,
        mesh=inner,
        in_specs=(
            P(DB, MP),
            P(DB, None, MP),
            P(DB, None),
            P(DB, None),
            P(None, MP),
            P(None, MP),
            P(DB, MP),
        ),
        out_specs=(P(DB, MP), P(DB, MP), P(DB, MP)),
        check_vma=False,
    )
```

```python
import functools

import jax
import jax.numpy as jnp
from jax import lax
from jax.experimental import pallas as pl
from jax.experimental.pallas import tpu as pltpu
from jax.sharding import Mesh
from jax.sharding import PartitionSpec as P

HEAD_DIM = 128
SPAN_LEN = 64
CHUNKS = (32, 32, 32, 32)
DB = ("z", "ylo", "core")
MP = ("x", "yhi")
VMEM_LIMIT = 60 * 1024 * 1024
SMALL = pl.CostEstimate(flops=1, bytes_accessed=1, transcendentals=0)
GROUPS = ((0, 2), (2, 8))
TARGETS = ((2, 1), (2, 0), (1, 1), (3, 1), (1, 0), (3, 0), (0, 1), (0, 0))


def ring(values, axis, shift, size):
    return lax.ppermute(values, axis, [(i, (i + shift) % size) for i in range(size)])


def tie(values, *others):
    return lax.optimization_barrier((values, *others))[0]


def run_copies(copies):
    for act in ("start", "wait"):
        for condition, source, target, sem in copies:
            copy = pltpu.make_async_copy(source, target, sem)
            pl.when(condition)(getattr(copy, act))


def run_copies(copies):
    for act in ("start", "wait"):
        for condition, source, target, sem in copies:
            copy = pltpu.make_async_copy(source, target, sem)
            pl.when(condition)(getattr(copy, act))


def planes_kernel(first, rows, place, one, two, three, own, across, packets, sems):
    chip = place[0] * 2 + place[1]
    count = one.shape[1] // 4
    copies = []
    for n, asked in enumerate((one, two, three)):
        base = (place[0] + n + 1) % 4 * 8
        for group in range(2):
            for i in range(count):
                here = asked[group, i] == chip
                mine = asked[group, count + i] == place[2]
                slot, rank = asked[group, 2 * count + i], asked[group, 3 * count + i]
                sem = sems.at[(n * 2 + group) * count + i]
                target = packets.at[base + group * 4 + rank]
                cut = (slot, pl.ds(first, rows))
                copies.append((here & mine, own.at[cut], target, sem))
                copies.append((here & ~mine, across.at[cut], target, sem))
    run_copies(copies)


def collect_kernel(first, rows, group, place, both, own, across, packets, *refs):
    output, sems = refs[-2:]
    count = both.shape[1] // 4
    copies = []
    for i in range(count):
        chip = both[group, i]
        plane = chip // 2
        side, near = chip % 2 == place[1], plane == place[0]
        mine = both[group, count + i] == place[2]
        slot, rank = both[group, 2 * count + i], both[group, 3 * count + i]
        sem, target = sems.at[i], output.at[i]
        cut = (slot, pl.ds(first, rows))
        copies.append((side & near & mine, own.at[cut], target, sem))
        copies.append((side & near & ~mine, across.at[cut], target, sem))
        copies.append((side & ~near, packets.at[plane * 8 + group * 4 + rank], target, sem))
        if group == 0:
            copies.append((~side, refs[0].at[i], target, sem))
    run_copies(copies)


def pack_kernel(first, rows, place, both, one, two, three, own, across, packets, sems):
    chip = place[0] * 2 + place[1]
    count = both.shape[1] // 4
    copies = []
    for n, asked in enumerate((both, one, two, three)):
        for group in range(2):
            base = ((place[0] + n) % 4 * 2 + (place[1] + group) % 2) * 4
            for i in range(count):
                here = asked[group, i] == chip
                mine = asked[group, count + i] == place[2]
                slot, rank = asked[group, 2 * count + i], asked[group, 3 * count + i]
                sem = sems.at[(n * 2 + group) * count + i]
                cut = (slot, pl.ds(first, rows))
                copies.append((here & mine, own.at[cut], packets.at[base + rank], sem))
                copies.append((here & ~mine, across.at[cut], packets.at[base + rank], sem))
    run_copies(copies)


def merge_kernel(wanted, packets, output, sems):
    count = wanted.shape[1] // 4
    copies = [
        pltpu.make_async_copy(
            packets.at[wanted[0, i] * 4 + wanted[0, 3 * count + i]], output.at[i], sems.at[i]
        )
        for i in range(count)
    ]
    for copy in copies:
        copy.start()
    for copy in copies:
        copy.wait()


def copies_call(kernel, name, shape, scalars, arrays, sems):
    return pl.pallas_call(
        kernel,
        name=name,
        out_shape=jax.ShapeDtypeStruct(shape, jnp.bfloat16),
        grid_spec=pltpu.PrefetchScalarGridSpec(
            num_scalar_prefetch=len(scalars),
            grid=(1,),
            in_specs=[pl.BlockSpec(memory_space=pl.ANY)] * len(arrays),
            out_specs=pl.BlockSpec(shape, lambda *_: (0, 0, 0)),
            scratch_shapes=[pltpu.SemaphoreType.DMA((sems,))],
        ),
        compiler_params=pltpu.CompilerParams(vmem_limit_bytes=VMEM_LIMIT),
        cost_estimate=SMALL,
    )(*scalars, *arrays)


def project_kernel(hops, first, starts, ends, joins, place, *refs):
    count = len(hops)
    pieces, key_weight = refs[:count], refs[count]
    refs = refs[count + 1:]
    if not starts:
        begun, refs = refs[0], refs[1:]
    refs = refs[sum(joins):]
    keys, mine, theirs, held, weights, piece_sems, weight_sems, mine_sems, their_sems = refs
    rows, depth = pieces[0].shape
    half = depth // 2
    columns = [
        pl.ds(pl.multiple_of(core * half, half), half) for core in (place[2], 1 - place[2])
    ]
    piece_reads, weight_reads, writes = [], [], []
    for n, (hop, side) in enumerate(hops):
        at = (place[3] + hop) % 4 * 2 + (place[4] + side) % 2
        cut = pl.ds(pl.multiple_of(at * depth, depth), depth)
        piece_reads.append(pltpu.make_async_copy(pieces[n], held.at[n], piece_sems.at[n]))
        weight_reads.append(
            pltpu.make_async_copy(key_weight.at[cut], weights.at[n], weight_sems.at[n])
        )
        writes.append((
            pltpu.make_async_copy(
                held.at[n, :, columns[0]], mine.at[at, pl.ds(first, rows)], mine_sems.at[n]
            ),
            pltpu.make_async_copy(
                held.at[n, :, columns[1]], theirs.at[at], their_sems.at[n]
            ),
        ))
    for n in range(count):
        piece_reads[n].start()
        weight_reads[n].start()
    total = None if starts else begun[...]
    for n in range(count):
        piece_reads[n].wait()
        for copy in writes[n]:
            copy.start()
        weight_reads[n].wait()
        part = jnp.dot(held[n], weights[n], preferred_element_type=jnp.float32)
        total = part if total is None else total + part
    keys[...] = total.astype(keys.dtype)
    for pair in writes:
        for copy in pair:
            copy.wait()


def project(place, pieces, hops, first, key_weight, mine=None, theirs=None, begun=None, ends=True):
    rows, depth = pieces[0].shape
    width = key_weight.shape[1]
    count = len(pieces)
    whole = pl.BlockSpec((rows, width), lambda step, place: (0, 0))
    anywhere = pl.BlockSpec(memory_space=pl.ANY)
    kind = jnp.bfloat16 if ends else jnp.float32
    operands = [place, *pieces, key_weight]
    in_specs = [anywhere] * (count + 1)
    aliases = {}
    if begun is not None:
        operands.append(begun)
        in_specs.append(whole)
    for n, joined in enumerate((mine, theirs)):
        if joined is not None:
            operands.append(joined)
            in_specs.append(anywhere)
            aliases[len(operands) - 1] = n + 1
    sems = pltpu.SemaphoreType.DMA((count,))
    return pl.pallas_call(
        functools.partial(
            project_kernel, hops, first, begun is None, ends,
            (mine is not None, theirs is not None),
        ),
        name="project",
        out_shape=(
            jax.ShapeDtypeStruct((rows, width), kind),
            jax.ShapeDtypeStruct((8, 8 * sum(CHUNKS), depth // 2), jnp.bfloat16),
            jax.ShapeDtypeStruct((8, rows, depth // 2), jnp.bfloat16),
        ),
        grid_spec=pltpu.PrefetchScalarGridSpec(
            num_scalar_prefetch=1,
            grid=(1,),
            in_specs=in_specs,
            out_specs=(whole, anywhere, anywhere),
            scratch_shapes=[
                pltpu.VMEM((count, rows, depth), jnp.bfloat16),
                pltpu.VMEM((count, depth, width), jnp.bfloat16),
                sems, sems, sems, sems,
            ],
        ),
        input_output_aliases=aliases,
        compiler_params=pltpu.CompilerParams(vmem_limit_bytes=VMEM_LIMIT),
        cost_estimate=SMALL,
    )(*operands)


def value_kernel(place, mine, *refs):
    step = pl.program_id(0)
    other_parts, (weight, values, total) = refs[:-3], refs[-3:]
    half = weight.shape[0] // 2
    near, away = [
        weight[pl.ds(pl.multiple_of(core * half, half), half), :]
        for core in (place[2], 1 - place[2])
    ]

    @pl.when(step == 0)
    def _():
        total[...] = jnp.zeros_like(total)

    total[...] += jnp.dot(mine[0], near, preferred_element_type=jnp.float32)
    start = 0
    for part in other_parts:
        rows = part.shape[1]
        total[start:start + rows] += jnp.dot(part[0], away, preferred_element_type=jnp.float32)
        start += rows

    @pl.when(step == 7)
    def _():
        values[...] = total[...].astype(values.dtype)


def project_values(place, mine, other_parts, value_weight):
    rows, half = mine.shape[1:]
    width = value_weight.shape[1]
    return pl.pallas_call(
        value_kernel,
        name="values",
        out_shape=jax.ShapeDtypeStruct((rows, width), jnp.bfloat16),
        grid_spec=pltpu.PrefetchScalarGridSpec(
            num_scalar_prefetch=1,
            grid=(8,),
            in_specs=[pl.BlockSpec((1, rows, half), lambda step, place: (step, 0, 0))]
            + [
                pl.BlockSpec((1, part.shape[1], half), lambda step, place: (step, 0, 0))
                for part in other_parts
            ]
            + [pl.BlockSpec((2 * half, width), lambda step, place: (step, 0))],
            out_specs=pl.BlockSpec((rows, width), lambda step, place: (0, 0)),
            scratch_shapes=[pltpu.VMEM((rows, width), jnp.float32)],
        ),
        compiler_params=pltpu.CompilerParams(vmem_limit_bytes=VMEM_LIMIT),
        cost_estimate=SMALL,
    )(place, mine, *other_parts, value_weight)


def span_rows(parts, span, low, high):
    pieces = []
    for part in parts:
        size = part.shape[0] // 4
        pieces.append(part[span * size:(span + 1) * size, low:high])
    return jnp.concatenate(pieces, axis=0)


def parts_of(rows, sizes):
    parts, start = [], 0
    for size in sizes:
        parts.append(rows.at[start:start + size])
        start += size
    return parts


def weigh_kernel(chunks, *refs):
    queries, cotangent = refs[0], refs[1]
    key_parts = refs[2:2 + chunks]
    chances, gradient, stacked = refs[2 + chunks:]
    width = queries.shape[1]
    scale = HEAD_DIM ** (-0.5)
    for span in range(4):
        tokens = slice(span * SPAN_LEN, (span + 1) * SPAN_LEN)
        for head in range(width // HEAD_DIM):
            low, high = head * HEAD_DIM, (head + 1) * HEAD_DIM
            keys = span_rows(key_parts, span, low, high)
            scores = lax.dot_general(
                queries[tokens, low:high], keys, (((1,), (1,)), ((), ())),
                preferred_element_type=jnp.float32,
            ) * scale
            raised = jnp.exp(scores - jnp.max(scores, axis=-1, keepdims=True))
            found = raised / jnp.sum(raised, axis=-1, keepdims=True)
            chances[span * (width // HEAD_DIM) + head] = found
            part = lax.dot_general(
                found.astype(jnp.bfloat16), cotangent[tokens, low:high], (((0,), (0,)), ((), ())),
                preferred_element_type=jnp.float32,
            ).astype(jnp.bfloat16)
            base, start = 0, 0
            for key_part in key_parts:
                size = key_part.shape[0] // 4
                at = base + span * size
                stacked[at:at + size, low:high] = part[start:start + size]
                start += size
                base += key_part.shape[0]
    gradient[...] = stacked[...].T


def weigh(queries, cotangent, key_parts):
    tokens, width = queries.shape
    rows = sum(part.shape[0] for part in key_parts)
    heads = width // HEAD_DIM
    vmem = pl.BlockSpec(memory_space=pltpu.VMEM)
    return pl.pallas_call(
        functools.partial(weigh_kernel, len(key_parts)),
        name="weigh",
        out_shape=(
            jax.ShapeDtypeStruct((4 * heads, SPAN_LEN, rows // 4), jnp.float32),
            jax.ShapeDtypeStruct((width, rows), jnp.bfloat16),
        ),
        in_specs=[vmem] * (2 + len(key_parts)),
        out_specs=(vmem, vmem),
        scratch_shapes=[pltpu.VMEM((rows, width), jnp.bfloat16)],
        compiler_params=pltpu.CompilerParams(vmem_limit_bytes=VMEM_LIMIT),
        cost_estimate=SMALL,
    )(queries, cotangent, *key_parts)


def attend_kernel(chunks, *refs):
    cotangent, chances, value_rows = refs[:3]
    key_parts = refs[3:3 + chunks]
    attended, query_grad = refs[3 + chunks:]
    value_parts = parts_of(value_rows, [part.shape[0] for part in key_parts])
    width = cotangent.shape[1]
    scale = HEAD_DIM ** (-0.5)
    for span in range(4):
        tokens = slice(span * SPAN_LEN, (span + 1) * SPAN_LEN)
        for head in range(width // HEAD_DIM):
            low, high = head * HEAD_DIM, (head + 1) * HEAD_DIM
            keys = span_rows(key_parts, span, low, high)
            values = span_rows(value_parts, span, low, high)
            found = chances[span * (width // HEAD_DIM) + head]
            attended[tokens, low:high] = jnp.dot(
                found.astype(jnp.bfloat16), values, preferred_element_type=jnp.float32
            ).astype(jnp.bfloat16)
            slope = lax.dot_general(
                cotangent[tokens, low:high], values, (((1,), (1,)), ((), ())),
                preferred_element_type=jnp.float32,
            )
            centre = jnp.sum(found * slope, axis=-1, keepdims=True)
            score_grad = (found * (slope - centre)).astype(jnp.bfloat16)
            query_grad[tokens, low:high] = (
                jnp.dot(score_grad, keys, preferred_element_type=jnp.float32) * scale
            ).astype(jnp.bfloat16)


def attend(cotangent, chances, key_parts, values):
    tokens, width = cotangent.shape
    rows = sum(part.shape[0] for part in key_parts)
    vmem = pl.BlockSpec(memory_space=pltpu.VMEM)
    return pl.pallas_call(
        functools.partial(attend_kernel, len(key_parts)),
        name="attend",
        out_shape=(
            jax.ShapeDtypeStruct((tokens, width), jnp.bfloat16),
            jax.ShapeDtypeStruct((tokens, width), jnp.bfloat16),
        ),
        in_specs=[vmem] * (3 + len(key_parts)),
        out_specs=(vmem, vmem),
        compiler_params=pltpu.CompilerParams(vmem_limit_bytes=VMEM_LIMIT),
        cost_estimate=SMALL,
    )(cotangent, chances, values, *key_parts)


def term_kernel(chunks, place, gradient, mine, their_gradient, *refs):
    step = pl.program_id(0)
    their_parts, outputs = refs[:chunks], refs[chunks:]
    total = jnp.dot(gradient[...], mine[0], preferred_element_type=jnp.float32)
    theirs, start = None, 0
    for part in their_parts:
        rows = part.shape[1]
        term = jnp.dot(
            their_gradient[:, start:start + rows], part[0], preferred_element_type=jnp.float32
        )
        theirs = term if theirs is None else theirs + term
        start += rows
    both = total.astype(jnp.bfloat16).astype(jnp.float32) + theirs.astype(jnp.bfloat16).astype(
        jnp.float32
    )
    for n, output in enumerate(outputs):
        @pl.when(step == n)
        def _():
            output[...] = both.astype(jnp.bfloat16)


def weight_terms(place, targets, gradient, mine, their_gradient, their_parts):
    count = len(targets)
    width, rows = gradient.shape
    half = mine.shape[2]

    def block_of(n, place):
        dz, dy = jnp.int32(targets[0][0]), jnp.int32(targets[0][1])
        for m in range(1, count):
            dz = jnp.where(n == m, targets[m][0], dz)
            dy = jnp.where(n == m, targets[m][1], dy)
        return (place[0] + dz) % 4 * 2 + (place[1] + dy) % 2, 0, 0

    whole = pl.BlockSpec((width, rows), lambda n, place: (0, 0))
    return pl.pallas_call(
        functools.partial(term_kernel, len(their_parts)),
        name="terms",
        out_shape=[jax.ShapeDtypeStruct((width, half), jnp.bfloat16)] * count,
        grid_spec=pltpu.PrefetchScalarGridSpec(
            num_scalar_prefetch=1,
            grid=(count,),
            in_specs=[whole, pl.BlockSpec((1, rows, half), block_of), whole]
            + [pl.BlockSpec((1, part.shape[1], half), block_of) for part in their_parts],
            out_specs=[pl.BlockSpec((width, half), lambda n, place: (0, 0))] * count,
        ),
        compiler_params=pltpu.CompilerParams(vmem_limit_bytes=VMEM_LIMIT),
        cost_estimate=SMALL,
    )(place, gradient, mine, their_gradient, *their_parts)


def total_kernel(*refs):
    output = refs[-1]
    total = refs[0][...].astype(jnp.float32)
    for block in refs[1:-1]:
        total += block[...].astype(jnp.float32)
    output[...] = total.T


def add_blocks(blocks):
    width, depth = blocks[0].shape
    vmem = pl.BlockSpec(memory_space=pltpu.VMEM)
    return pl.pallas_call(
        total_kernel,
        name="total",
        out_shape=jax.ShapeDtypeStruct((depth, width), jnp.float32),
        in_specs=[vmem] * len(blocks),
        out_specs=vmem,
        compiler_params=pltpu.CompilerParams(vmem_limit_bytes=VMEM_LIMIT),
        cost_estimate=SMALL,
    )(*blocks)


def per_device(
    queries, database, neighbor_owner, neighbor_slot, key_weight, value_weight, cotangent
):
    z, ylo, core = lax.axis_index("z"), lax.axis_index("ylo"), lax.axis_index("core")
    x, yhi = lax.axis_index("x"), lax.axis_index("yhi")
    place = jnp.stack([z, ylo, core, x, yhi]).astype(jnp.int32)
    count = neighbor_owner.shape[0] * neighbor_owner.shape[1]
    width = database.shape[2]
    owners = neighbor_owner.reshape(1, count)
    chips = owners // 2
    earlier = jnp.arange(count)[:, None] > jnp.arange(count)[None, :]
    ranks = jnp.sum((chips.reshape(count, 1) == chips) & earlier, axis=1).reshape(1, count)
    wanted = jnp.concatenate(
        [chips, owners % 2, neighbor_slot.reshape(1, count), ranks.astype(jnp.int32)], axis=1
    )
    both = jnp.concatenate([wanted, ring(wanted, "ylo", 1, 2)], axis=0)
    asked = [ring(both, "z", -n, 4) for n in (1, 2, 3)]
    across = ring(database, "core", 1, 2)

    last = len(CHUNKS) - 1
    firsts = [sum(CHUNKS[:k]) for k in range(last + 1)]

    near_hops = ((0, 0), (3, 0), (1, 0), (0, 1), (3, 1), (1, 1))
    far_hops = ((2, 0), (2, 1))

    def shape(k):
        return count, CHUNKS[k], width

    def hand(k, packets, *after):
        given = copies_call(
            functools.partial(collect_kernel, firsts[k], CHUNKS[k], 1), "hand", shape(k),
            [tie(place, *after), both], [database, across, packets], count,
        )
        return given, ring(given, "ylo", 1, 2)

    def merge(k, packets, given, *after):
        return copies_call(
            functools.partial(collect_kernel, firsts[k], CHUNKS[k], 0), "merge", shape(k),
            [tie(place, *after), both], [database, across, packets, given], count,
        )

    def spread(own, *after):
        own = own.reshape(-1, width)
        left, right = ring(own, "x", 1, 4), ring(own, "x", -1, 4)
        other = ring(own, "yhi", 1, 2)
        sent = tie(other, left, right, *after)
        near = (own, left, right, other, ring(sent, "x", 1, 4), ring(sent, "x", -1, 4))
        return near, (near[1], near[5])

    def pass_on(ends):
        return ring(ends[0], "x", 1, 4), ring(ends[1], "x", -1, 4)

    def send_planes(packets, *after):
        return lax.all_to_all(tie(packets, *after), "z", 0, 0, tiled=True)

    packets = copies_call(
        functools.partial(pack_kernel, 0, CHUNKS[0]), "pack", (32, CHUNKS[0], width),
        [place, both, *asked], [database, across], 8 * count,
    )
    arrived = lax.all_to_all(packets, ("z", "ylo"), 0, 0, tiled=True)
    planes = [packets]
    for k in range(1, last + 1):
        planes.append(
            copies_call(
                functools.partial(planes_kernel, firsts[k], CHUNKS[k]), "planes",
                (32, CHUNKS[k], width), [tie(place, planes[-1]), *asked], [database, across],
                6 * count,
            )
        )
    own = copies_call(merge_kernel, "merge", shape(0), [tie(wanted, planes[-1])], [arrived], count)
    by_plane = send_planes(planes[1], own)
    near, ends = spread(own)
    key_parts, their_parts, sent_parts, mine, waiting = [], [], [], None, None

    def finish(k, ready, pieces, hops, **begun):
        keys, mine_now, theirs = project(
            ready, pieces, hops, firsts[k] * count, key_weight, mine, **begun
        )
        key_parts.append(keys)
        sent_parts.append(theirs)
        their_parts.append(ring(theirs, "core", 1, 2))
        return mine_now

    for k in range(1, last + 1):
        handed, given = hand(k, by_plane, *(near[1:] if k == 1 else near[1:4]))
        here = by_plane
        if k < last:
            by_plane = send_planes(planes[k + 1], handed)
        far = pass_on(ends)
        if waiting is not None:
            mine = finish(k - 2, tie(place, handed), waiting, near_hops + far_hops)
        waiting = (*near, *far)
        own = merge(k, here, given, *near[4:])
        near, ends = spread(own, *key_parts[-1:])
    mine = finish(last - 1, tie(place, near[3]), waiting, near_hops + far_hops)
    far = pass_on(ends)
    begun, mine, theirs = project(
        tie(place, key_parts[-1]), near, near_hops, firsts[-1] * count, key_weight, mine,
        ends=False,
    )
    mine = finish(last, place, far, far_hops, theirs=theirs, begun=begun)

    chances, gradient = weigh(queries, cotangent, key_parts)
    their_gradient = ring(gradient, "core", 1, 2)
    totals = []
    summed = ()
    for low, high in GROUPS:
        blocks = weight_terms(
            tie(place, *summed), TARGETS[low:high], gradient, mine, their_gradient, their_parts
        )
        summed = blocks[:1]
        for (dz, dy), block in zip(TARGETS[low:high], blocks):
            if (dz, dy) != (0, 0):
                block = lax.ppermute(
                    block, ("z", "ylo"),
                    [
                        (a * 2 + b, (a + dz) % 4 * 2 + (b + dy) % 2)
                        for a in range(4) for b in range(2)
                    ],
                )
            totals.append(block)
    values = project_values(tie(place, *summed, *totals[:GROUPS[0][1]]), mine, sent_parts, value_weight)
    attended, query_grad = attend(cotangent, chances, key_parts, values)
    value_weight_grad = add_blocks([*totals[:-1], tie(totals[-1], attended)])
    return attended, query_grad, value_weight_grad


def solution(mesh):
    inner = Mesh(mesh.devices.reshape(4, 2, 2, 4, 2), (*DB, *MP))
    return jax.shard_map(
        per_device,
        mesh=inner,
        in_specs=(
            P(DB, MP),
            P(DB, None, MP),
            P(DB, None),
            P(DB, None),
            P(None, MP),
            P(None, MP),
            P(DB, MP),
        ),
        out_specs=(P(DB, MP), P(DB, MP), P(DB, MP)),
        check_vma=False,
    )
```

```python
import functools

import jax
import jax.numpy as jnp
from jax import lax
from jax.experimental import pallas as pl
from jax.experimental.pallas import tpu as pltpu
from jax.sharding import Mesh
from jax.sharding import PartitionSpec as P

HEAD_DIM = 128
SPAN_LEN = 64
CHUNKS = (64, 64)
DB = ("z", "ylo", "core")
MP = ("x", "yhi")
VMEM_LIMIT = 60 * 1024 * 1024
SMALL = pl.CostEstimate(flops=1, bytes_accessed=1, transcendentals=0)


def ring(values, axis, shift, size):
    return lax.ppermute(values, axis, [(i, (i + shift) % size) for i in range(size)])


def tie(values, *others):
    return lax.optimization_barrier((values, *others))[0]


def run_copies(copies):
    for act in ("start", "wait"):
        for condition, source, target, sem in copies:
            copy = pltpu.make_async_copy(source, target, sem)
            pl.when(condition)(getattr(copy, act))


def run_copies(copies):
    for act in ("start", "wait"):
        for condition, source, target, sem in copies:
            copy = pltpu.make_async_copy(source, target, sem)
            pl.when(condition)(getattr(copy, act))


def planes_kernel(first, rows, place, one, two, three, own, across, packets, sems):
    chip = place[0] * 2 + place[1]
    count = one.shape[1] // 4
    copies = []
    for n, asked in enumerate((one, two, three)):
        base = (place[0] + n + 1) % 4 * 8
        for group in range(2):
            for i in range(count):
                here = asked[group, i] == chip
                mine = asked[group, count + i] == place[2]
                slot, rank = asked[group, 2 * count + i], asked[group, 3 * count + i]
                sem = sems.at[(n * 2 + group) * count + i]
                target = packets.at[base + group * 4 + rank]
                cut = (slot, pl.ds(first, rows))
                copies.append((here & mine, own.at[cut], target, sem))
                copies.append((here & ~mine, across.at[cut], target, sem))
    run_copies(copies)


def collect_kernel(first, rows, group, place, both, own, across, packets, *refs):
    output, sems = refs[-2:]
    count = both.shape[1] // 4
    copies = []
    for i in range(count):
        chip = both[group, i]
        plane = chip // 2
        side, near = chip % 2 == place[1], plane == place[0]
        mine = both[group, count + i] == place[2]
        slot, rank = both[group, 2 * count + i], both[group, 3 * count + i]
        sem, target = sems.at[i], output.at[i]
        cut = (slot, pl.ds(first, rows))
        copies.append((side & near & mine, own.at[cut], target, sem))
        copies.append((side & near & ~mine, across.at[cut], target, sem))
        copies.append((side & ~near, packets.at[plane * 8 + group * 4 + rank], target, sem))
        if group == 0:
            copies.append((~side, refs[0].at[i], target, sem))
    run_copies(copies)


def pack_kernel(first, rows, place, both, one, two, three, own, across, packets, sems):
    chip = place[0] * 2 + place[1]
    count = both.shape[1] // 4
    copies = []
    for n, asked in enumerate((both, one, two, three)):
        for group in range(2):
            base = ((place[0] + n) % 4 * 2 + (place[1] + group) % 2) * 4
            for i in range(count):
                here = asked[group, i] == chip
                mine = asked[group, count + i] == place[2]
                slot, rank = asked[group, 2 * count + i], asked[group, 3 * count + i]
                sem = sems.at[(n * 2 + group) * count + i]
                cut = (slot, pl.ds(first, rows))
                copies.append((here & mine, own.at[cut], packets.at[base + rank], sem))
                copies.append((here & ~mine, across.at[cut], packets.at[base + rank], sem))
    run_copies(copies)


def merge_kernel(wanted, packets, output, sems):
    count = wanted.shape[1] // 4
    copies = [
        pltpu.make_async_copy(
            packets.at[wanted[0, i] * 4 + wanted[0, 3 * count + i]], output.at[i], sems.at[i]
        )
        for i in range(count)
    ]
    for copy in copies:
        copy.start()
    for copy in copies:
        copy.wait()


def copies_call(kernel, name, shape, scalars, arrays, sems):
    return pl.pallas_call(
        kernel,
        name=name,
        out_shape=jax.ShapeDtypeStruct(shape, jnp.bfloat16),
        grid_spec=pltpu.PrefetchScalarGridSpec(
            num_scalar_prefetch=len(scalars),
            grid=(1,),
            in_specs=[pl.BlockSpec(memory_space=pl.ANY)] * len(arrays),
            out_specs=pl.BlockSpec(shape, lambda *_: (0, 0, 0)),
            scratch_shapes=[pltpu.SemaphoreType.DMA((sems,))],
        ),
        compiler_params=pltpu.CompilerParams(vmem_limit_bytes=VMEM_LIMIT),
        cost_estimate=SMALL,
    )(*scalars, *arrays)


def project_kernel(hops, first, starts, ends, joins, valued, place, *refs):
    count = len(hops)
    pieces, matrices = refs[:count], refs[count:count + 1 + valued]
    refs = refs[count + 1 + valued:]
    if not starts:
        begun, refs = refs[:1 + valued], refs[1 + valued:]
    refs = refs[sum(joins):]
    keys, mine, theirs, refs = refs[0], refs[1], refs[2], refs[3:]
    results = (keys, *refs[:valued])
    held, weights, piece_sems, weight_sems, mine_sems, their_sems = refs[valued:]
    rows, depth = pieces[0].shape
    half = depth // 2
    columns = [
        pl.ds(pl.multiple_of(core * half, half), half) for core in (place[2], 1 - place[2])
    ]
    piece_reads, weight_reads, writes = [], [], []
    for n, (hop, side) in enumerate(hops):
        at = (place[3] + hop * (2 * place[2] - 1) + 4) % 4 * 2 + (place[4] + side) % 2
        cut = pl.ds(pl.multiple_of(at * depth, depth), depth)
        piece_reads.append(pltpu.make_async_copy(pieces[n], held.at[n], piece_sems.at[n]))
        weight_reads.append([
            pltpu.make_async_copy(matrix.at[cut], weights.at[m, n], weight_sems.at[m, n])
            for m, matrix in enumerate(matrices)
        ])
        writes.append((
            pltpu.make_async_copy(
                held.at[n, :, columns[0]], mine.at[at, pl.ds(first, rows)], mine_sems.at[n]
            ),
            pltpu.make_async_copy(
                held.at[n, :, columns[1]], theirs.at[at], their_sems.at[n]
            ),
        ))
    for n in range(count):
        piece_reads[n].start()
        for copy in weight_reads[n]:
            copy.start()
    totals = [None] * len(matrices) if starts else [sums[...] for sums in begun]
    for n in range(count):
        piece_reads[n].wait()
        for copy in writes[n]:
            copy.start()
        for m in range(len(matrices)):
            weight_reads[n][m].wait()
            part = jnp.dot(held[n], weights[m, n], preferred_element_type=jnp.float32)
            totals[m] = part if totals[m] is None else totals[m] + part
    for result, total in zip(results, totals):
        result[...] = total.astype(result.dtype)
    for pair in writes:
        for copy in pair:
            copy.wait()


def project(place, pieces, hops, first, matrices, mine=None, theirs=None, begun=None, ends=True):
    rows, depth = pieces[0].shape
    width = matrices[0].shape[1]
    count = len(pieces)
    valued = len(matrices) - 1
    whole = pl.BlockSpec((rows, width), lambda step, place: (0, 0))
    anywhere = pl.BlockSpec(memory_space=pl.ANY)
    kind = jnp.bfloat16 if ends else jnp.float32
    operands = [place, *pieces, *matrices]
    in_specs = [anywhere] * (count + 1 + valued)
    aliases = {}
    if begun is not None:
        operands.extend(begun)
        in_specs.extend([whole] * len(begun))
    for n, joined in enumerate((mine, theirs)):
        if joined is not None:
            operands.append(joined)
            in_specs.append(anywhere)
            aliases[len(operands) - 1] = n + 1
    sems = pltpu.SemaphoreType.DMA((count,))
    result = jax.ShapeDtypeStruct((rows, width), kind)
    return pl.pallas_call(
        functools.partial(
            project_kernel, hops, first, begun is None, ends,
            (mine is not None, theirs is not None), valued,
        ),
        name="project",
        out_shape=(
            result,
            jax.ShapeDtypeStruct((8, 8 * sum(CHUNKS), depth // 2), jnp.bfloat16),
            jax.ShapeDtypeStruct((8, rows, depth // 2), jnp.bfloat16),
            *[result] * valued,
        ),
        grid_spec=pltpu.PrefetchScalarGridSpec(
            num_scalar_prefetch=1,
            grid=(1,),
            in_specs=in_specs,
            out_specs=(whole, anywhere, anywhere, *[whole] * valued),
            scratch_shapes=[
                pltpu.VMEM((count, rows, depth), jnp.bfloat16),
                pltpu.VMEM((1 + valued, count, depth, width), jnp.bfloat16),
                sems, pltpu.SemaphoreType.DMA((1 + valued, count)), sems, sems,
            ],
        ),
        input_output_aliases=aliases,
        compiler_params=pltpu.CompilerParams(vmem_limit_bytes=VMEM_LIMIT),
        cost_estimate=SMALL,
    )(*operands)


def span_rows(parts, span, low, high):
    pieces = []
    for part in parts:
        size = part.shape[0] // 4
        pieces.append(part[span * size:(span + 1) * size, low:high])
    return jnp.concatenate(pieces, axis=0)


def weigh_kernel(chunks, *refs):
    queries, cotangent = refs[0], refs[1]
    key_parts = refs[2:2 + chunks]
    chances, gradient, stacked = refs[2 + chunks:]
    width = queries.shape[1]
    scale = HEAD_DIM ** (-0.5)
    for span in range(4):
        tokens = slice(span * SPAN_LEN, (span + 1) * SPAN_LEN)
        for head in range(width // HEAD_DIM):
            low, high = head * HEAD_DIM, (head + 1) * HEAD_DIM
            keys = span_rows(key_parts, span, low, high)
            scores = lax.dot_general(
                queries[tokens, low:high], keys, (((1,), (1,)), ((), ())),
                preferred_element_type=jnp.float32,
            ) * scale
            raised = jnp.exp(scores - jnp.max(scores, axis=-1, keepdims=True))
            found = raised / jnp.sum(raised, axis=-1, keepdims=True)
            chances[span * (width // HEAD_DIM) + head] = found
            part = lax.dot_general(
                found.astype(jnp.bfloat16), cotangent[tokens, low:high], (((0,), (0,)), ((), ())),
                preferred_element_type=jnp.float32,
            ).astype(jnp.bfloat16)
            base, start = 0, 0
            for key_part in key_parts:
                size = key_part.shape[0] // 4
                at = base + span * size
                stacked[at:at + size, low:high] = part[start:start + size]
                start += size
                base += key_part.shape[0]
    gradient[...] = stacked[...].T


def weigh(queries, cotangent, key_parts):
    tokens, width = queries.shape
    rows = sum(part.shape[0] for part in key_parts)
    heads = width // HEAD_DIM
    vmem = pl.BlockSpec(memory_space=pltpu.VMEM)
    return pl.pallas_call(
        functools.partial(weigh_kernel, len(key_parts)),
        name="weigh",
        out_shape=(
            jax.ShapeDtypeStruct((4 * heads, SPAN_LEN, rows // 4), jnp.float32),
            jax.ShapeDtypeStruct((width, rows), jnp.bfloat16),
        ),
        in_specs=[vmem] * (2 + len(key_parts)),
        out_specs=(vmem, vmem),
        scratch_shapes=[pltpu.VMEM((rows, width), jnp.bfloat16)],
        compiler_params=pltpu.CompilerParams(vmem_limit_bytes=VMEM_LIMIT),
        cost_estimate=SMALL,
    )(queries, cotangent, *key_parts)


def attend_kernel(chunks, *refs):
    cotangent, chances = refs[:2]
    key_parts, value_parts = refs[2:2 + chunks], refs[2 + chunks:2 + 2 * chunks]
    attended, query_grad = refs[2 + 2 * chunks:]
    width = cotangent.shape[1]
    scale = HEAD_DIM ** (-0.5)
    for span in range(4):
        tokens = slice(span * SPAN_LEN, (span + 1) * SPAN_LEN)
        for head in range(width // HEAD_DIM):
            low, high = head * HEAD_DIM, (head + 1) * HEAD_DIM
            keys = span_rows(key_parts, span, low, high)
            values = span_rows(value_parts, span, low, high)
            found = chances[span * (width // HEAD_DIM) + head]
            attended[tokens, low:high] = jnp.dot(
                found.astype(jnp.bfloat16), values, preferred_element_type=jnp.float32
            ).astype(jnp.bfloat16)
            slope = lax.dot_general(
                cotangent[tokens, low:high], values, (((1,), (1,)), ((), ())),
                preferred_element_type=jnp.float32,
            )
            centre = jnp.sum(found * slope, axis=-1, keepdims=True)
            score_grad = (found * (slope - centre)).astype(jnp.bfloat16)
            query_grad[tokens, low:high] = (
                jnp.dot(score_grad, keys, preferred_element_type=jnp.float32) * scale
            ).astype(jnp.bfloat16)


def attend(cotangent, chances, key_parts, value_parts):
    tokens, width = cotangent.shape
    rows = sum(part.shape[0] for part in key_parts)
    vmem = pl.BlockSpec(memory_space=pltpu.VMEM)
    return pl.pallas_call(
        functools.partial(attend_kernel, len(key_parts)),
        name="attend",
        out_shape=(
            jax.ShapeDtypeStruct((tokens, width), jnp.bfloat16),
            jax.ShapeDtypeStruct((tokens, width), jnp.bfloat16),
        ),
        in_specs=[vmem] * (2 + 2 * len(key_parts)),
        out_specs=(vmem, vmem),
        compiler_params=pltpu.CompilerParams(vmem_limit_bytes=VMEM_LIMIT),
        cost_estimate=SMALL,
    )(cotangent, chances, *key_parts, *value_parts)


def term_kernel(chunks, sizes, adds, place, gradient, mine, their_gradient, *refs):
    step = pl.program_id(0)
    their_parts, outputs = refs[:chunks], refs[chunks + adds:]
    total = jnp.dot(gradient[...], mine[0], preferred_element_type=jnp.float32)
    theirs, start = None, 0
    for part in their_parts:
        rows = part.shape[1]
        term = jnp.dot(
            their_gradient[:, start:start + rows], part[0], preferred_element_type=jnp.float32
        )
        theirs = term if theirs is None else theirs + term
        start += rows
    both = total.astype(jnp.bfloat16).astype(jnp.float32) + theirs.astype(jnp.bfloat16).astype(
        jnp.float32
    )
    low = 0
    for n, (size, output) in enumerate(zip(sizes, outputs)):
        @pl.when((step >= low) & (step < low + size))
        def _():
            result = both
            if adds and n == 0:
                result = both + refs[chunks][0].astype(jnp.float32)
            output[0] = result.astype(jnp.bfloat16)
        low += size


def weight_terms(place, targets, sizes, gradient, mine, their_gradient, their_parts, arrived=()):
    count = len(targets)
    width, rows = gradient.shape
    half = mine.shape[2]

    def block_of(n, place):
        dz, dy = jnp.int32(targets[0][0]), jnp.int32(targets[0][1])
        for m in range(1, count):
            dz = jnp.where(n == m, targets[m][0], dz)
            dy = jnp.where(n == m, targets[m][1], dy)
        return (place[0] + dz) % 4 * 2 + (place[1] + dy) % 2, 0, 0

    def result_of(low, size):
        return pl.BlockSpec(
            (1, width, half), lambda n, place: (jnp.clip(n - low, 0, size - 1), 0, 0)
        )

    whole = pl.BlockSpec((width, rows), lambda n, place: (0, 0))
    return pl.pallas_call(
        functools.partial(term_kernel, len(their_parts), sizes, len(arrived)),
        name="terms",
        out_shape=[jax.ShapeDtypeStruct((size, width, half), jnp.bfloat16) for size in sizes],
        grid_spec=pltpu.PrefetchScalarGridSpec(
            num_scalar_prefetch=1,
            grid=(count,),
            in_specs=[whole, pl.BlockSpec((1, rows, half), block_of), whole]
            + [pl.BlockSpec((1, part.shape[1], half), block_of) for part in their_parts]
            + [pl.BlockSpec((1, width, half), lambda n, place: (0, 0, 0))] * len(arrived),
            out_specs=[
                result_of(sum(sizes[:n]), size) for n, size in enumerate(sizes)
            ],
        ),
        compiler_params=pltpu.CompilerParams(vmem_limit_bytes=VMEM_LIMIT),
        cost_estimate=SMALL,
    )(place, gradient, mine, their_gradient, *their_parts, *arrived)


def total_kernel(*refs):
    output = refs[-1]
    total = refs[0][0].astype(jnp.float32)
    for block in refs[1:-1]:
        total += block[0].astype(jnp.float32)
    output[...] = total.T


def add_blocks(blocks):
    width, depth = blocks[0].shape[1:]
    return pl.pallas_call(
        total_kernel,
        name="total",
        out_shape=jax.ShapeDtypeStruct((depth, width), jnp.float32),
        grid=(1,),
        in_specs=[pl.BlockSpec((1, width, depth), lambda n: (0, 0, 0))] * len(blocks),
        out_specs=pl.BlockSpec((depth, width), lambda n: (0, 0)),
        compiler_params=pltpu.CompilerParams(vmem_limit_bytes=VMEM_LIMIT),
        cost_estimate=SMALL,
    )(*blocks)


def per_device(
    queries, database, neighbor_owner, neighbor_slot, key_weight, value_weight, cotangent
):
    z, ylo, core = lax.axis_index("z"), lax.axis_index("ylo"), lax.axis_index("core")
    x, yhi = lax.axis_index("x"), lax.axis_index("yhi")
    place = jnp.stack([z, ylo, core, x, yhi]).astype(jnp.int32)
    count = neighbor_owner.shape[0] * neighbor_owner.shape[1]
    width = database.shape[2]
    owners = neighbor_owner.reshape(1, count)
    chips = owners // 2
    earlier = jnp.arange(count)[:, None] > jnp.arange(count)[None, :]
    ranks = jnp.sum((chips.reshape(count, 1) == chips) & earlier, axis=1).reshape(1, count)
    wanted = jnp.concatenate(
        [chips, owners % 2, neighbor_slot.reshape(1, count), ranks.astype(jnp.int32)], axis=1
    )
    both = jnp.concatenate([wanted, ring(wanted, "ylo", 1, 2)], axis=0)
    asked = [ring(both, "z", -n, 4) for n in (1, 2, 3)]
    across = ring(database, "core", 1, 2)

    firsts = [sum(CHUNKS[:k]) for k in range(len(CHUNKS))]

    near_hops = ((0, 0), (1, 0), (-1, 0), (0, 1), (1, 1), (-1, 1))
    far_hops = ((2, 0), (2, 1))

    def shape(k):
        return count, CHUNKS[k], width

    def hand(k, packets, *after):
        given = copies_call(
            functools.partial(collect_kernel, firsts[k], CHUNKS[k], 1), "hand", shape(k),
            [tie(place, *after), both], [database, across, packets], count,
        )
        return given, ring(given, "ylo", 1, 2)

    def merge(k, packets, given, *after):
        return copies_call(
            functools.partial(collect_kernel, firsts[k], CHUNKS[k], 0), "merge", shape(k),
            [tie(place, *after), both], [database, across, packets, given], count,
        )

    def along(values, way):
        steps = (way, -way)
        return lax.ppermute(
            values, ("core", "x"),
            [(c * 4 + i, c * 4 + (i + steps[c]) % 4) for c in range(2) for i in range(4)],
        )

    def spread_sides(own):
        own = own.reshape(-1, width)
        ahead, behind = along(own, 1), along(own, -1)
        other = ring(own, "yhi", 1, 2)
        return (own, ahead, behind, other), tie(other, ahead, behind)

    def spread(own):
        near, sent = spread_sides(own)
        return *near, along(sent, 1), along(sent, -1)

    def send_planes(packets, *after):
        return lax.all_to_all(tie(packets, *after), "z", 0, 0, tiled=True)

    packets = copies_call(
        functools.partial(pack_kernel, 0, CHUNKS[0]), "pack", (32, CHUNKS[0], width),
        [place, both, *asked], [database, across], 8 * count,
    )
    arrived = lax.all_to_all(packets, ("z", "ylo"), 0, 0, tiled=True)
    planes = [packets]
    for k in range(1, len(CHUNKS)):
        planes.append(
            copies_call(
                functools.partial(planes_kernel, firsts[k], CHUNKS[k]), "planes",
                (32, CHUNKS[k], width), [tie(place, planes[-1]), *asked], [database, across],
                6 * count,
            )
        )
    own = copies_call(merge_kernel, "merge", shape(0), [tie(wanted, planes[-1])], [arrived], count)
    by_plane = send_planes(planes[1], own)
    near = spread(own)
    far = (along(near[1], 1),)
    handed, given = hand(1, by_plane, *near[1:4])
    far += (along(tie(near[5], handed), -1),)
    own = merge(1, by_plane, given, *near[4:], far[0])
    matrices = (key_weight, value_weight)
    keys, mine, theirs, values = project(
        tie(place, own), (*near, *far), near_hops + far_hops, 0, matrices
    )
    near, other = spread_sides(own)
    far = along(tie(near[1], keys), 1)
    steps = [(near, near_hops[:4]), ((far,), far_hops[:1])]
    begun, last_theirs = None, None
    for n in range(3):
        if n == 1:
            sent = tie(other, far, key_sum)
            steps.append((
                (along(sent, 1), along(sent, -1), ring(far, "yhi", 1, 2)),
                near_hops[4:] + far_hops[1:],
            ))
        pieces, hops = steps[n]
        key_sum, mine, last_theirs, value_sum = project(
            place, pieces, hops, firsts[1] * count, matrices, mine, last_theirs, begun, n == 2
        )
        begun = key_sum, value_sum
    key_parts, value_parts = [keys, key_sum], [values, value_sum]
    their_parts = [ring(theirs, "core", 1, 2), ring(last_theirs, "core", 1, 2)]

    chances, gradient = weigh(queries, cotangent, key_parts)
    their_gradient = ring(gradient, "core", 1, 2)
    def terms(targets, sizes, arrived=(), after=()):
        return weight_terms(
            tie(place, *after), targets, sizes, gradient, mine, their_gradient, their_parts,
            arrived,
        )

    ahead, behind = terms(((1, 0), (1, 1), (3, 0), (3, 1)), (2, 2))
    corner, = terms(((2, 1),), (1,), (), (behind,))
    beside, here = terms(((0, 1), (0, 0)), (1, 1), (), (corner,))
    far, = terms(((2, 0),), (1,), (ring(corner, "ylo", 1, 2),), (here,))
    beside = tie(beside, far)
    ahead, behind = ring(ahead, "z", 1, 4), ring(behind, "z", -1, 4)
    far = ring(far, "z", 2, 4)
    beside = beside.astype(jnp.float32) + ahead[1:] + behind[1:]
    beside = ring(beside.astype(jnp.bfloat16), "ylo", 1, 2)
    attended, query_grad = attend(cotangent, chances, key_parts, value_parts)
    value_weight_grad = add_blocks(
        [ahead, behind, far, here, tie(beside, attended)]
    )
    return attended, query_grad, value_weight_grad


def solution(mesh):
    inner = Mesh(mesh.devices.reshape(4, 2, 2, 4, 2), (*DB, *MP))
    return jax.shard_map(
        per_device,
        mesh=inner,
        in_specs=(
            P(DB, MP),
            P(DB, None, MP),
            P(DB, None),
            P(DB, None),
            P(None, MP),
            P(None, MP),
            P(DB, MP),
        ),
        out_specs=(P(DB, MP), P(DB, MP), P(DB, MP)),
        check_vma=False,
    )
```

```python
import functools

import jax
import jax.numpy as jnp
from jax import lax
from jax.experimental import pallas as pl
from jax.experimental.pallas import tpu as pltpu
from jax.sharding import Mesh
from jax.sharding import PartitionSpec as P

HEAD_DIM = 128
SPAN_LEN = 64
CHUNKS = (64, 64)
DB = ("z", "ylo", "core")
MP = ("x", "yhi")
VMEM_LIMIT = 60 * 1024 * 1024
SMALL = pl.CostEstimate(flops=1, bytes_accessed=1, transcendentals=0)


def ring(values, axis, shift, size):
    return lax.ppermute(values, axis, [(i, (i + shift) % size) for i in range(size)])


def tie(values, *others):
    return lax.optimization_barrier((values, *others))[0]


def run_copies(copies):
    for act in ("start", "wait"):
        for condition, source, target, sem in copies:
            copy = pltpu.make_async_copy(source, target, sem)
            pl.when(condition)(getattr(copy, act))


def run_copies(copies):
    for act in ("start", "wait"):
        for condition, source, target, sem in copies:
            copy = pltpu.make_async_copy(source, target, sem)
            pl.when(condition)(getattr(copy, act))


def planes_kernel(first, rows, place, one, two, three, own, across, packets, sems):
    chip = place[0] * 2 + place[1]
    count = one.shape[1] // 4
    copies = []
    for n, asked in enumerate((one, two, three)):
        base = (place[0] + n + 1) % 4 * 8
        for group in range(2):
            for i in range(count):
                here = asked[group, i] == chip
                mine = asked[group, count + i] == place[2]
                slot, rank = asked[group, 2 * count + i], asked[group, 3 * count + i]
                sem = sems.at[(n * 2 + group) * count + i]
                target = packets.at[base + group * 4 + rank]
                cut = (slot, pl.ds(first, rows))
                copies.append((here & mine, own.at[cut], target, sem))
                copies.append((here & ~mine, across.at[cut], target, sem))
    run_copies(copies)


def collect_kernel(first, rows, group, place, both, own, across, packets, *refs):
    output, sems = refs[-2:]
    count = both.shape[1] // 4
    copies = []
    for i in range(count):
        chip = both[group, i]
        plane = chip // 2
        side, near = chip % 2 == place[1], plane == place[0]
        mine = both[group, count + i] == place[2]
        slot, rank = both[group, 2 * count + i], both[group, 3 * count + i]
        sem, target = sems.at[i], output.at[i]
        cut = (slot, pl.ds(first, rows))
        copies.append((side & near & mine, own.at[cut], target, sem))
        copies.append((side & near & ~mine, across.at[cut], target, sem))
        copies.append((side & ~near, packets.at[plane * 8 + group * 4 + rank], target, sem))
        if group == 0:
            copies.append((~side, refs[0].at[i], target, sem))
    run_copies(copies)


def pack_kernel(first, rows, place, both, one, two, three, own, across, packets, sems):
    chip = place[0] * 2 + place[1]
    count = both.shape[1] // 4
    copies = []
    for n, asked in enumerate((both, one, two, three)):
        for group in range(2):
            base = ((place[0] + n) % 4 * 2 + (place[1] + group) % 2) * 4
            for i in range(count):
                here = asked[group, i] == chip
                mine = asked[group, count + i] == place[2]
                slot, rank = asked[group, 2 * count + i], asked[group, 3 * count + i]
                sem = sems.at[(n * 2 + group) * count + i]
                cut = (slot, pl.ds(first, rows))
                copies.append((here & mine, own.at[cut], packets.at[base + rank], sem))
                copies.append((here & ~mine, across.at[cut], packets.at[base + rank], sem))
    run_copies(copies)


def merge_kernel(wanted, packets, output, sems):
    count = wanted.shape[1] // 4
    copies = [
        pltpu.make_async_copy(
            packets.at[wanted[0, i] * 4 + wanted[0, 3 * count + i]], output.at[i], sems.at[i]
        )
        for i in range(count)
    ]
    for copy in copies:
        copy.start()
    for copy in copies:
        copy.wait()


def copies_call(kernel, name, shape, scalars, arrays, sems):
    return pl.pallas_call(
        kernel,
        name=name,
        out_shape=jax.ShapeDtypeStruct(shape, jnp.bfloat16),
        grid_spec=pltpu.PrefetchScalarGridSpec(
            num_scalar_prefetch=len(scalars),
            grid=(1,),
            in_specs=[pl.BlockSpec(memory_space=pl.ANY)] * len(arrays),
            out_specs=pl.BlockSpec(shape, lambda *_: (0, 0, 0)),
            scratch_shapes=[pltpu.SemaphoreType.DMA((sems,))],
        ),
        compiler_params=pltpu.CompilerParams(vmem_limit_bytes=VMEM_LIMIT),
        cost_estimate=SMALL,
    )(*scalars, *arrays)


def project_kernel(hops, first, starts, ends, joins, valued, place, *refs):
    count = len(hops)
    pieces, matrices = refs[:count], refs[count:count + 1 + valued]
    refs = refs[count + 1 + valued:]
    if not starts:
        begun, refs = refs[:1 + valued], refs[1 + valued:]
    refs = refs[sum(joins):]
    keys, mine, theirs, refs = refs[0], refs[1], refs[2], refs[3:]
    results = (keys, *refs[:valued])
    held, weights, piece_sems, weight_sems, mine_sems, their_sems = refs[valued:]
    rows, depth = pieces[0].shape
    half = depth // 2
    columns = [
        pl.ds(pl.multiple_of(core * half, half), half) for core in (place[2], 1 - place[2])
    ]
    piece_reads, weight_reads, writes = [], [], []
    for n, (hop, side) in enumerate(hops):
        at = (place[3] + hop * (2 * place[2] - 1) + 4) % 4 * 2 + (place[4] + side) % 2
        cut = pl.ds(pl.multiple_of(at * depth, depth), depth)
        piece_reads.append(pltpu.make_async_copy(pieces[n], held.at[n], piece_sems.at[n]))
        weight_reads.append([
            pltpu.make_async_copy(matrix.at[cut], weights.at[m, n], weight_sems.at[m, n])
            for m, matrix in enumerate(matrices)
        ])
        writes.append((
            pltpu.make_async_copy(
                held.at[n, :, columns[0]], mine.at[at, pl.ds(first, rows)], mine_sems.at[n]
            ),
            pltpu.make_async_copy(
                held.at[n, :, columns[1]], theirs.at[at], their_sems.at[n]
            ),
        ))
    for n in range(count):
        piece_reads[n].start()
        for copy in weight_reads[n]:
            copy.start()
    totals = [None] * len(matrices) if starts else [sums[...] for sums in begun]
    for n in range(count):
        piece_reads[n].wait()
        for copy in writes[n]:
            copy.start()
        for m in range(len(matrices)):
            weight_reads[n][m].wait()
            part = jnp.dot(held[n], weights[m, n], preferred_element_type=jnp.float32)
            totals[m] = part if totals[m] is None else totals[m] + part
    for result, total in zip(results, totals):
        result[...] = total.astype(result.dtype)
    for pair in writes:
        for copy in pair:
            copy.wait()


def project(place, pieces, hops, first, matrices, mine=None, theirs=None, begun=None, ends=True):
    rows, depth = pieces[0].shape
    width = matrices[0].shape[1]
    count = len(pieces)
    valued = len(matrices) - 1
    whole = pl.BlockSpec((rows, width), lambda step, place: (0, 0))
    anywhere = pl.BlockSpec(memory_space=pl.ANY)
    kind = jnp.bfloat16 if ends else jnp.float32
    operands = [place, *pieces, *matrices]
    in_specs = [anywhere] * (count + 1 + valued)
    aliases = {}
    if begun is not None:
        operands.extend(begun)
        in_specs.extend([whole] * len(begun))
    for n, joined in enumerate((mine, theirs)):
        if joined is not None:
            operands.append(joined)
            in_specs.append(anywhere)
            aliases[len(operands) - 1] = n + 1
    sems = pltpu.SemaphoreType.DMA((count,))
    result = jax.ShapeDtypeStruct((rows, width), kind)
    return pl.pallas_call(
        functools.partial(
            project_kernel, hops, first, begun is None, ends,
            (mine is not None, theirs is not None), valued,
        ),
        name="project",
        out_shape=(
            result,
            jax.ShapeDtypeStruct((8, 8 * sum(CHUNKS), depth // 2), jnp.bfloat16),
            jax.ShapeDtypeStruct((8, rows, depth // 2), jnp.bfloat16),
            *[result] * valued,
        ),
        grid_spec=pltpu.PrefetchScalarGridSpec(
            num_scalar_prefetch=1,
            grid=(1,),
            in_specs=in_specs,
            out_specs=(whole, anywhere, anywhere, *[whole] * valued),
            scratch_shapes=[
                pltpu.VMEM((count, rows, depth), jnp.bfloat16),
                pltpu.VMEM((1 + valued, count, depth, width), jnp.bfloat16),
                sems, pltpu.SemaphoreType.DMA((1 + valued, count)), sems, sems,
            ],
        ),
        input_output_aliases=aliases,
        compiler_params=pltpu.CompilerParams(vmem_limit_bytes=VMEM_LIMIT * 2 // 3),
        cost_estimate=SMALL,
    )(*operands)


def span_rows(parts, span, low, high):
    pieces = []
    for part in parts:
        size = part.shape[0] // 4
        pieces.append(part[span * size:(span + 1) * size, low:high])
    return jnp.concatenate(pieces, axis=0)


def weigh_kernel(chunks, *refs):
    queries, cotangent = refs[0], refs[1]
    key_parts = refs[2:2 + chunks]
    chances, gradient, stacked = refs[2 + chunks:]
    width = queries.shape[1]
    scale = HEAD_DIM ** (-0.5)
    for span in range(4):
        tokens = slice(span * SPAN_LEN, (span + 1) * SPAN_LEN)
        for head in range(width // HEAD_DIM):
            low, high = head * HEAD_DIM, (head + 1) * HEAD_DIM
            keys = span_rows(key_parts, span, low, high)
            scores = lax.dot_general(
                queries[tokens, low:high], keys, (((1,), (1,)), ((), ())),
                preferred_element_type=jnp.float32,
            ) * scale
            raised = jnp.exp(scores - jnp.max(scores, axis=-1, keepdims=True))
            found = raised / jnp.sum(raised, axis=-1, keepdims=True)
            chances[span * (width // HEAD_DIM) + head] = found
            part = lax.dot_general(
                found.astype(jnp.bfloat16), cotangent[tokens, low:high], (((0,), (0,)), ((), ())),
                preferred_element_type=jnp.float32,
            ).astype(jnp.bfloat16)
            base, start = 0, 0
            for key_part in key_parts:
                size = key_part.shape[0] // 4
                at = base + span * size
                stacked[at:at + size, low:high] = part[start:start + size]
                start += size
                base += key_part.shape[0]
    gradient[...] = stacked[...].T


def weigh(queries, cotangent, key_parts):
    tokens, width = queries.shape
    rows = sum(part.shape[0] for part in key_parts)
    heads = width // HEAD_DIM
    vmem = pl.BlockSpec(memory_space=pltpu.VMEM)
    return pl.pallas_call(
        functools.partial(weigh_kernel, len(key_parts)),
        name="weigh",
        out_shape=(
            jax.ShapeDtypeStruct((4 * heads, SPAN_LEN, rows // 4), jnp.float32),
            jax.ShapeDtypeStruct((width, rows), jnp.bfloat16),
        ),
        in_specs=[vmem] * (2 + len(key_parts)),
        out_specs=(vmem, vmem),
        scratch_shapes=[pltpu.VMEM((rows, width), jnp.bfloat16)],
        compiler_params=pltpu.CompilerParams(vmem_limit_bytes=VMEM_LIMIT // 2),
        cost_estimate=SMALL,
    )(queries, cotangent, *key_parts)


def attend_kernel(chunks, *refs):
    cotangent, chances = refs[:2]
    key_parts, value_parts = refs[2:2 + chunks], refs[2 + chunks:2 + 2 * chunks]
    attended, query_grad = refs[2 + 2 * chunks:]
    width = cotangent.shape[1]
    scale = HEAD_DIM ** (-0.5)
    for span in range(4):
        tokens = slice(span * SPAN_LEN, (span + 1) * SPAN_LEN)
        for head in range(width // HEAD_DIM):
            low, high = head * HEAD_DIM, (head + 1) * HEAD_DIM
            keys = span_rows(key_parts, span, low, high)
            values = span_rows(value_parts, span, low, high)
            found = chances[span * (width // HEAD_DIM) + head]
            attended[tokens, low:high] = jnp.dot(
                found.astype(jnp.bfloat16), values, preferred_element_type=jnp.float32
            ).astype(jnp.bfloat16)
            slope = lax.dot_general(
                cotangent[tokens, low:high], values, (((1,), (1,)), ((), ())),
                preferred_element_type=jnp.float32,
            )
            centre = jnp.sum(found * slope, axis=-1, keepdims=True)
            score_grad = (found * (slope - centre)).astype(jnp.bfloat16)
            query_grad[tokens, low:high] = (
                jnp.dot(score_grad, keys, preferred_element_type=jnp.float32) * scale
            ).astype(jnp.bfloat16)


def attend(cotangent, chances, key_parts, value_parts):
    tokens, width = cotangent.shape
    rows = sum(part.shape[0] for part in key_parts)
    vmem = pl.BlockSpec(memory_space=pltpu.VMEM)
    return pl.pallas_call(
        functools.partial(attend_kernel, len(key_parts)),
        name="attend",
        out_shape=(
            jax.ShapeDtypeStruct((tokens, width), jnp.bfloat16),
            jax.ShapeDtypeStruct((tokens, width), jnp.bfloat16),
        ),
        in_specs=[vmem] * (2 + 2 * len(key_parts)),
        out_specs=(vmem, vmem),
        compiler_params=pltpu.CompilerParams(vmem_limit_bytes=VMEM_LIMIT // 2),
        cost_estimate=SMALL,
    )(cotangent, chances, *key_parts, *value_parts)


def term_kernel(chunks, sizes, adds, place, gradient, mine, their_gradient, *refs):
    step = pl.program_id(0)
    their_parts, outputs = refs[:chunks], refs[chunks + adds:]
    total = jnp.dot(gradient[...], mine[0], preferred_element_type=jnp.float32)
    theirs, start = None, 0
    for part in their_parts:
        rows = part.shape[1]
        term = jnp.dot(
            their_gradient[:, start:start + rows], part[0], preferred_element_type=jnp.float32
        )
        theirs = term if theirs is None else theirs + term
        start += rows
    both = total.astype(jnp.bfloat16).astype(jnp.float32) + theirs.astype(jnp.bfloat16).astype(
        jnp.float32
    )
    low = 0
    for n, (size, output) in enumerate(zip(sizes, outputs)):
        @pl.when((step >= low) & (step < low + size))
        def _():
            result = both
            if adds and n == 0:
                result = both + refs[chunks][0].astype(jnp.float32)
            output[0] = result.astype(jnp.bfloat16)
        low += size


def weight_terms(place, targets, sizes, gradient, mine, their_gradient, their_parts, arrived=()):
    count = len(targets)
    width, rows = gradient.shape
    half = mine.shape[2]

    def block_of(n, place):
        dz, dy = jnp.int32(targets[0][0]), jnp.int32(targets[0][1])
        for m in range(1, count):
            dz = jnp.where(n == m, targets[m][0], dz)
            dy = jnp.where(n == m, targets[m][1], dy)
        return (place[0] + dz) % 4 * 2 + (place[1] + dy) % 2, 0, 0

    def result_of(low, size):
        return pl.BlockSpec(
            (1, width, half), lambda n, place: (jnp.clip(n - low, 0, size - 1), 0, 0)
        )

    whole = pl.BlockSpec((width, rows), lambda n, place: (0, 0))
    return pl.pallas_call(
        functools.partial(term_kernel, len(their_parts), sizes, len(arrived)),
        name="terms",
        out_shape=[jax.ShapeDtypeStruct((size, width, half), jnp.bfloat16) for size in sizes],
        grid_spec=pltpu.PrefetchScalarGridSpec(
            num_scalar_prefetch=1,
            grid=(count,),
            in_specs=[whole, pl.BlockSpec((1, rows, half), block_of), whole]
            + [pl.BlockSpec((1, part.shape[1], half), block_of) for part in their_parts]
            + [pl.BlockSpec((1, width, half), lambda n, place: (0, 0, 0))] * len(arrived),
            out_specs=[
                result_of(sum(sizes[:n]), size) for n, size in enumerate(sizes)
            ],
        ),
        compiler_params=pltpu.CompilerParams(vmem_limit_bytes=VMEM_LIMIT // 2),
        cost_estimate=SMALL,
    )(place, gradient, mine, their_gradient, *their_parts, *arrived)


def total_kernel(*refs):
    output = refs[-1]
    total = refs[0][0].astype(jnp.float32)
    for block in refs[1:-1]:
        total += block[0].astype(jnp.float32)
    output[...] = total.T


def add_blocks(blocks):
    width, depth = blocks[0].shape[1:]
    return pl.pallas_call(
        total_kernel,
        name="total",
        out_shape=jax.ShapeDtypeStruct((depth, width), jnp.float32),
        grid=(1,),
        in_specs=[pl.BlockSpec((1, width, depth), lambda n: (0, 0, 0))] * len(blocks),
        out_specs=pl.BlockSpec((depth, width), lambda n: (0, 0)),
        compiler_params=pltpu.CompilerParams(vmem_limit_bytes=VMEM_LIMIT // 2),
        cost_estimate=SMALL,
    )(*blocks)


def per_device(
    queries, database, neighbor_owner, neighbor_slot, key_weight, value_weight, cotangent
):
    z, ylo, core = lax.axis_index("z"), lax.axis_index("ylo"), lax.axis_index("core")
    x, yhi = lax.axis_index("x"), lax.axis_index("yhi")
    place = jnp.stack([z, ylo, core, x, yhi]).astype(jnp.int32)
    count = neighbor_owner.shape[0] * neighbor_owner.shape[1]
    width = database.shape[2]
    owners = neighbor_owner.reshape(1, count)
    chips = owners // 2
    earlier = jnp.arange(count)[:, None] > jnp.arange(count)[None, :]
    ranks = jnp.sum((chips.reshape(count, 1) == chips) & earlier, axis=1).reshape(1, count)
    wanted = jnp.concatenate(
        [chips, owners % 2, neighbor_slot.reshape(1, count), ranks.astype(jnp.int32)], axis=1
    )
    both = jnp.concatenate([wanted, ring(wanted, "ylo", 1, 2)], axis=0)
    asked = [ring(both, "z", -n, 4) for n in (1, 2, 3)]
    across = ring(database, "core", 1, 2)

    firsts = [sum(CHUNKS[:k]) for k in range(len(CHUNKS))]

    near_hops = ((0, 0), (1, 0), (-1, 0), (0, 1), (1, 1), (-1, 1))
    far_hops = ((2, 0), (2, 1))

    def shape(k):
        return count, CHUNKS[k], width

    def hand(k, packets, *after):
        given = copies_call(
            functools.partial(collect_kernel, firsts[k], CHUNKS[k], 1), "hand", shape(k),
            [tie(place, *after), both], [database, across, packets], count,
        )
        return given, ring(given, "ylo", 1, 2)

    def merge(k, packets, given, *after):
        return copies_call(
            functools.partial(collect_kernel, firsts[k], CHUNKS[k], 0), "merge", shape(k),
            [tie(place, *after), both], [database, across, packets, given], count,
        )

    def along(values, way):
        steps = (way, -way)
        return lax.ppermute(
            values, ("core", "x"),
            [(c * 4 + i, c * 4 + (i + steps[c]) % 4) for c in range(2) for i in range(4)],
        )

    def spread_sides(own):
        own = own.reshape(-1, width)
        ahead, behind = along(own, 1), along(own, -1)
        other = ring(own, "yhi", 1, 2)
        return (own, ahead, behind, other), tie(other, ahead, behind)

    def spread(own):
        near, sent = spread_sides(own)
        return *near, along(sent, 1), along(sent, -1)

    def send_planes(packets, *after):
        return lax.all_to_all(tie(packets, *after), "z", 0, 0, tiled=True)

    packets = copies_call(
        functools.partial(pack_kernel, 0, CHUNKS[0]), "pack", (32, CHUNKS[0], width),
        [place, both, *asked], [database, across], 8 * count,
    )
    arrived = lax.all_to_all(packets, ("z", "ylo"), 0, 0, tiled=True)
    planes = [packets]
    for k in range(1, len(CHUNKS)):
        planes.append(
            copies_call(
                functools.partial(planes_kernel, firsts[k], CHUNKS[k]), "planes",
                (32, CHUNKS[k], width), [tie(place, planes[-1]), *asked], [database, across],
                6 * count,
            )
        )
    own = copies_call(merge_kernel, "merge", shape(0), [tie(wanted, planes[-1])], [arrived], count)
    by_plane = send_planes(planes[1], own)
    near = spread(own)
    far = (along(near[1], 1),)
    handed, given = hand(1, by_plane, *near[1:4])
    far += (along(tie(near[5], handed), -1),)
    own = merge(1, by_plane, given, *near[4:], far[0])
    matrices = (key_weight, value_weight)
    keys, mine, theirs, values = project(
        tie(place, own), (*near, *far), near_hops + far_hops, 0, matrices
    )
    near, other = spread_sides(own)
    far = along(tie(near[1], keys), 1)
    steps = [(near, near_hops[:4]), ((far,), far_hops[:1])]
    begun, last_theirs = None, None
    for n in range(3):
        if n == 1:
            sent = tie(other, far, key_sum)
            steps.append((
                (along(sent, 1), along(sent, -1), ring(far, "yhi", 1, 2)),
                near_hops[4:] + far_hops[1:],
            ))
        pieces, hops = steps[n]
        key_sum, mine, last_theirs, value_sum = project(
            place, pieces, hops, firsts[1] * count, matrices, mine, last_theirs, begun, n == 2
        )
        begun = key_sum, value_sum
    key_parts, value_parts = [keys, key_sum], [values, value_sum]
    their_parts = [ring(theirs, "core", 1, 2), ring(last_theirs, "core", 1, 2)]

    chances, gradient = weigh(queries, cotangent, key_parts)
    their_gradient = ring(gradient, "core", 1, 2)
    def terms(targets, sizes, arrived=(), after=()):
        return weight_terms(
            tie(place, *after), targets, sizes, gradient, mine, their_gradient, their_parts,
            arrived,
        )

    ahead, behind = terms(((1, 0), (1, 1), (3, 0), (3, 1)), (2, 2))
    corner, = terms(((2, 1),), (1,), (), (behind,))
    beside, here = terms(((0, 1), (0, 0)), (1, 1), (), (corner,))
    far, = terms(((2, 0),), (1,), (ring(corner, "ylo", 1, 2),), (here,))
    beside = tie(beside, far)
    ahead, behind = ring(ahead, "z", 1, 4), ring(behind, "z", -1, 4)
    far = ring(far, "z", 2, 4)
    beside = beside.astype(jnp.float32) + ahead[1:] + behind[1:]
    beside = ring(beside.astype(jnp.bfloat16), "ylo", 1, 2)
    attended, query_grad = attend(cotangent, chances, key_parts, value_parts)
    value_weight_grad = add_blocks(
        [ahead, behind, far, here, tie(beside, attended)]
    )
    return attended, query_grad, value_weight_grad


def solution(mesh):
    inner = Mesh(mesh.devices.reshape(4, 2, 2, 4, 2), (*DB, *MP))
    return jax.shard_map(
        per_device,
        mesh=inner,
        in_specs=(
            P(DB, MP),
            P(DB, None, MP),
            P(DB, None),
            P(DB, None),
            P(None, MP),
            P(None, MP),
            P(DB, MP),
        ),
        out_specs=(P(DB, MP), P(DB, MP), P(DB, MP)),
        check_vma=False,
    )
```

```python
import functools

import jax
import jax.numpy as jnp
from jax import lax
from jax.experimental import pallas as pl
from jax.experimental.pallas import tpu as pltpu
from jax.sharding import Mesh
from jax.sharding import PartitionSpec as P

HEAD_DIM = 128
SPAN_LEN = 64
CHUNKS = (64, 64)
DB = ("z", "ylo", "core")
MP = ("x", "yhi")
VMEM_LIMIT = 60 * 1024 * 1024
SMALL = pl.CostEstimate(flops=1, bytes_accessed=1, transcendentals=0)


def ring(values, axis, shift, size):
    return lax.ppermute(values, axis, [(i, (i + shift) % size) for i in range(size)])


def tie(values, *others):
    return lax.optimization_barrier((values, *others))[0]


def run_copies(copies):
    for act in ("start", "wait"):
        for condition, source, target, sem in copies:
            copy = pltpu.make_async_copy(source, target, sem)
            pl.when(condition)(getattr(copy, act))


def run_copies(copies):
    for act in ("start", "wait"):
        for condition, source, target, sem in copies:
            copy = pltpu.make_async_copy(source, target, sem)
            pl.when(condition)(getattr(copy, act))


def planes_kernel(first, rows, place, one, two, three, own, across, packets, sems):
    chip = place[0] * 2 + place[1]
    count = one.shape[1] // 4
    copies = []
    for n, asked in enumerate((one, two, three)):
        base = (place[0] + n + 1) % 4 * 8
        for group in range(2):
            for i in range(count):
                here = asked[group, i] == chip
                mine = asked[group, count + i] == place[2]
                slot, rank = asked[group, 2 * count + i], asked[group, 3 * count + i]
                sem = sems.at[(n * 2 + group) * count + i]
                target = packets.at[base + group * 4 + rank]
                cut = (slot, pl.ds(first, rows))
                copies.append((here & mine, own.at[cut], target, sem))
                copies.append((here & ~mine, across.at[cut], target, sem))
    run_copies(copies)


def collect_kernel(first, rows, group, place, both, own, across, packets, *refs):
    output, sems = refs[-2:]
    count = both.shape[1] // 4
    copies = []
    for i in range(count):
        chip = both[group, i]
        plane = chip // 2
        side, near = chip % 2 == place[1], plane == place[0]
        mine = both[group, count + i] == place[2]
        slot, rank = both[group, 2 * count + i], both[group, 3 * count + i]
        sem, target = sems.at[i], output.at[i]
        cut = (slot, pl.ds(first, rows))
        copies.append((side & near & mine, own.at[cut], target, sem))
        copies.append((side & near & ~mine, across.at[cut], target, sem))
        copies.append((side & ~near, packets.at[plane * 8 + group * 4 + rank], target, sem))
        if group == 0:
            copies.append((~side, refs[0].at[i], target, sem))
    run_copies(copies)


def pack_kernel(first, rows, place, both, one, two, three, own, across, packets, sems):
    chip = place[0] * 2 + place[1]
    count = both.shape[1] // 4
    copies = []
    for n, asked in enumerate((both, one, two, three)):
        for group in range(2):
            base = ((place[0] + n) % 4 * 2 + (place[1] + group) % 2) * 4
            for i in range(count):
                here = asked[group, i] == chip
                mine = asked[group, count + i] == place[2]
                slot, rank = asked[group, 2 * count + i], asked[group, 3 * count + i]
                sem = sems.at[(n * 2 + group) * count + i]
                cut = (slot, pl.ds(first, rows))
                copies.append((here & mine, own.at[cut], packets.at[base + rank], sem))
                copies.append((here & ~mine, across.at[cut], packets.at[base + rank], sem))
    run_copies(copies)


def merge_kernel(wanted, packets, output, sems):
    count = wanted.shape[1] // 4
    copies = [
        pltpu.make_async_copy(
            packets.at[wanted[0, i] * 4 + wanted[0, 3 * count + i]], output.at[i], sems.at[i]
        )
        for i in range(count)
    ]
    for copy in copies:
        copy.start()
    for copy in copies:
        copy.wait()


def copies_call(kernel, name, shape, scalars, arrays, sems):
    return pl.pallas_call(
        kernel,
        name=name,
        out_shape=jax.ShapeDtypeStruct(shape, jnp.bfloat16),
        grid_spec=pltpu.PrefetchScalarGridSpec(
            num_scalar_prefetch=len(scalars),
            grid=(1,),
            in_specs=[pl.BlockSpec(memory_space=pl.ANY)] * len(arrays),
            out_specs=pl.BlockSpec(shape, lambda *_: (0, 0, 0)),
            scratch_shapes=[pltpu.SemaphoreType.DMA((sems,))],
        ),
        compiler_params=pltpu.CompilerParams(vmem_limit_bytes=VMEM_LIMIT),
        cost_estimate=SMALL,
    )(*scalars, *arrays)


def project_kernel(hops, first, starts, ends, joins, valued, place, *refs):
    count = len(hops)
    pieces, matrices = refs[:count], refs[count:count + 1 + valued]
    refs = refs[count + 1 + valued:]
    if not starts:
        begun, refs = refs[:1 + valued], refs[1 + valued:]
    refs = refs[sum(joins):]
    keys, mine, theirs, refs = refs[0], refs[1], refs[2], refs[3:]
    results = (keys, *refs[:valued])
    held, weights, piece_sems, weight_sems, mine_sems, their_sems = refs[valued:]
    rows, depth = pieces[0].shape
    half = depth // 2
    columns = [
        pl.ds(pl.multiple_of(core * half, half), half) for core in (place[2], 1 - place[2])
    ]
    piece_reads, weight_reads, writes = [], [], []
    for n, (hop, side) in enumerate(hops):
        at = (place[3] + hop * (2 * place[2] - 1) + 4) % 4 * 2 + (place[4] + side) % 2
        cut = pl.ds(pl.multiple_of(at * depth, depth), depth)
        piece_reads.append(pltpu.make_async_copy(pieces[n], held.at[n], piece_sems.at[n]))
        weight_reads.append([
            pltpu.make_async_copy(matrix.at[cut], weights.at[m, n], weight_sems.at[m, n])
            for m, matrix in enumerate(matrices)
        ])
        writes.append((
            pltpu.make_async_copy(
                held.at[n, :, columns[0]], mine.at[at, pl.ds(first, rows)], mine_sems.at[n]
            ),
            pltpu.make_async_copy(
                held.at[n, :, columns[1]], theirs.at[at], their_sems.at[n]
            ),
        ))
    for n in range(count):
        piece_reads[n].start()
        for copy in weight_reads[n]:
            copy.start()
    totals = [None] * len(matrices) if starts else [sums[...] for sums in begun]
    for n in range(count):
        piece_reads[n].wait()
        for copy in writes[n]:
            copy.start()
        for m in range(len(matrices)):
            weight_reads[n][m].wait()
            part = jnp.dot(held[n], weights[m, n], preferred_element_type=jnp.float32)
            totals[m] = part if totals[m] is None else totals[m] + part
    for result, total in zip(results, totals):
        result[...] = total.astype(result.dtype)
    for pair in writes:
        for copy in pair:
            copy.wait()


def project(place, pieces, hops, first, matrices, mine=None, theirs=None, begun=None, ends=True):
    rows, depth = pieces[0].shape
    width = matrices[0].shape[1]
    count = len(pieces)
    valued = len(matrices) - 1
    whole = pl.BlockSpec((rows, width), lambda step, place: (0, 0))
    anywhere = pl.BlockSpec(memory_space=pl.ANY)
    kind = jnp.bfloat16 if ends else jnp.float32
    operands = [place, *pieces, *matrices]
    in_specs = [anywhere] * (count + 1 + valued)
    aliases = {}
    if begun is not None:
        operands.extend(begun)
        in_specs.extend([whole] * len(begun))
    for n, joined in enumerate((mine, theirs)):
        if joined is not None:
            operands.append(joined)
            in_specs.append(anywhere)
            aliases[len(operands) - 1] = n + 1
    sems = pltpu.SemaphoreType.DMA((count,))
    result = jax.ShapeDtypeStruct((rows, width), kind)
    return pl.pallas_call(
        functools.partial(
            project_kernel, hops, first, begun is None, ends,
            (mine is not None, theirs is not None), valued,
        ),
        name="project",
        out_shape=(
            result,
            jax.ShapeDtypeStruct((8, 8 * sum(CHUNKS), depth // 2), jnp.bfloat16),
            jax.ShapeDtypeStruct((8, rows, depth // 2), jnp.bfloat16),
            *[result] * valued,
        ),
        grid_spec=pltpu.PrefetchScalarGridSpec(
            num_scalar_prefetch=1,
            grid=(1,),
            in_specs=in_specs,
            out_specs=(whole, anywhere, anywhere, *[whole] * valued),
            scratch_shapes=[
                pltpu.VMEM((count, rows, depth), jnp.bfloat16),
                pltpu.VMEM((1 + valued, count, depth, width), jnp.bfloat16),
                sems, pltpu.SemaphoreType.DMA((1 + valued, count)), sems, sems,
            ],
        ),
        input_output_aliases=aliases,
        compiler_params=pltpu.CompilerParams(vmem_limit_bytes=VMEM_LIMIT * 2 // 3),
        cost_estimate=SMALL,
    )(*operands)


def span_rows(parts, span, low, high):
    pieces = []
    for part in parts:
        size = part.shape[0] // 4
        pieces.append(part[span * size:(span + 1) * size, low:high])
    return jnp.concatenate(pieces, axis=0)


def weigh_kernel(chunks, *refs):
    queries, cotangent = refs[0], refs[1]
    key_parts = refs[2:2 + chunks]
    chances, gradient, stacked = refs[2 + chunks:]
    width = queries.shape[1]
    scale = HEAD_DIM ** (-0.5)
    for span in range(4):
        tokens = slice(span * SPAN_LEN, (span + 1) * SPAN_LEN)
        for head in range(width // HEAD_DIM):
            low, high = head * HEAD_DIM, (head + 1) * HEAD_DIM
            keys = span_rows(key_parts, span, low, high)
            scores = lax.dot_general(
                queries[tokens, low:high], keys, (((1,), (1,)), ((), ())),
                preferred_element_type=jnp.float32,
            ) * scale
            raised = jnp.exp(scores - jnp.max(scores, axis=-1, keepdims=True))
            found = raised / jnp.sum(raised, axis=-1, keepdims=True)
            chances[span * (width // HEAD_DIM) + head] = found
            part = lax.dot_general(
                found.astype(jnp.bfloat16), cotangent[tokens, low:high], (((0,), (0,)), ((), ())),
                preferred_element_type=jnp.float32,
            ).astype(jnp.bfloat16)
            base, start = 0, 0
            for key_part in key_parts:
                size = key_part.shape[0] // 4
                at = base + span * size
                stacked[at:at + size, low:high] = part[start:start + size]
                start += size
                base += key_part.shape[0]
    gradient[...] = stacked[...].T


def weigh(queries, cotangent, key_parts):
    tokens, width = queries.shape
    rows = sum(part.shape[0] for part in key_parts)
    heads = width // HEAD_DIM
    vmem = pl.BlockSpec(memory_space=pltpu.VMEM)
    return pl.pallas_call(
        functools.partial(weigh_kernel, len(key_parts)),
        name="weigh",
        out_shape=(
            jax.ShapeDtypeStruct((4 * heads, SPAN_LEN, rows // 4), jnp.float32),
            jax.ShapeDtypeStruct((width, rows), jnp.bfloat16),
        ),
        in_specs=[vmem] * (2 + len(key_parts)),
        out_specs=(vmem, vmem),
        scratch_shapes=[pltpu.VMEM((rows, width), jnp.bfloat16)],
        compiler_params=pltpu.CompilerParams(vmem_limit_bytes=VMEM_LIMIT // 2),
        cost_estimate=SMALL,
    )(queries, cotangent, *key_parts)


def attend_kernel(chunks, *refs):
    cotangent, chances = refs[:2]
    key_parts, value_parts = refs[2:2 + chunks], refs[2 + chunks:2 + 2 * chunks]
    attended, query_grad = refs[2 + 2 * chunks:]
    width = cotangent.shape[1]
    scale = HEAD_DIM ** (-0.5)
    for span in range(4):
        tokens = slice(span * SPAN_LEN, (span + 1) * SPAN_LEN)
        for head in range(width // HEAD_DIM):
            low, high = head * HEAD_DIM, (head + 1) * HEAD_DIM
            keys = span_rows(key_parts, span, low, high)
            values = span_rows(value_parts, span, low, high)
            found = chances[span * (width // HEAD_DIM) + head]
            attended[tokens, low:high] = jnp.dot(
                found.astype(jnp.bfloat16), values, preferred_element_type=jnp.float32
            ).astype(jnp.bfloat16)
            slope = lax.dot_general(
                cotangent[tokens, low:high], values, (((1,), (1,)), ((), ())),
                preferred_element_type=jnp.float32,
            )
            centre = jnp.sum(found * slope, axis=-1, keepdims=True)
            score_grad = (found * (slope - centre)).astype(jnp.bfloat16)
            query_grad[tokens, low:high] = (
                jnp.dot(score_grad, keys, preferred_element_type=jnp.float32) * scale
            ).astype(jnp.bfloat16)


def attend(cotangent, chances, key_parts, value_parts):
    tokens, width = cotangent.shape
    rows = sum(part.shape[0] for part in key_parts)
    vmem = pl.BlockSpec(memory_space=pltpu.VMEM)
    return pl.pallas_call(
        functools.partial(attend_kernel, len(key_parts)),
        name="attend",
        out_shape=(
            jax.ShapeDtypeStruct((tokens, width), jnp.bfloat16),
            jax.ShapeDtypeStruct((tokens, width), jnp.bfloat16),
        ),
        in_specs=[vmem] * (2 + 2 * len(key_parts)),
        out_specs=(vmem, vmem),
        compiler_params=pltpu.CompilerParams(vmem_limit_bytes=VMEM_LIMIT // 2),
        cost_estimate=SMALL,
    )(cotangent, chances, *key_parts, *value_parts)


def own_kernel(place, gradient, mine, output):
    output[0] = jnp.dot(gradient[...], mine[0], preferred_element_type=jnp.float32).astype(
        jnp.bfloat16
    )


def own_terms(place, targets, gradient, mine):
    count = len(targets)
    width, rows = gradient.shape
    half = mine.shape[2]
    return pl.pallas_call(
        own_kernel,
        name="own",
        out_shape=jax.ShapeDtypeStruct((count, width, half), jnp.bfloat16),
        grid_spec=pltpu.PrefetchScalarGridSpec(
            num_scalar_prefetch=1,
            grid=(count,),
            in_specs=[
                pl.BlockSpec((width, rows), lambda n, place: (0, 0)),
                pl.BlockSpec((1, rows, half), functools.partial(block_of, targets)),
            ],
            out_specs=pl.BlockSpec((1, width, half), lambda n, place: (n, 0, 0)),
        ),
        compiler_params=pltpu.CompilerParams(vmem_limit_bytes=VMEM_LIMIT // 2),
        cost_estimate=SMALL,
    )(place, gradient, mine)


def block_of(targets, n, place):
    dz, dy = jnp.int32(targets[0][0]), jnp.int32(targets[0][1])
    for m in range(1, len(targets)):
        dz = jnp.where(n == m, targets[m][0], dz)
        dy = jnp.where(n == m, targets[m][1], dy)
    return (place[0] + dz) % 4 * 2 + (place[1] + dy) % 2, 0, 0


def term_kernel(chunks, sizes, adds, shared, place, *refs):
    step = pl.program_id(0)
    if shared:
        total, their_gradient, refs = refs[0][0], refs[1], refs[2:]
    else:
        gradient, mine, their_gradient, refs = *refs[:3], refs[3:]
        total = jnp.dot(gradient[...], mine[0], preferred_element_type=jnp.float32)
    their_parts, outputs = refs[:chunks], refs[chunks + adds:]
    theirs, start = None, 0
    for part in their_parts:
        rows = part.shape[1]
        term = jnp.dot(
            their_gradient[:, start:start + rows], part[0], preferred_element_type=jnp.float32
        )
        theirs = term if theirs is None else theirs + term
        start += rows
    both = total.astype(jnp.bfloat16).astype(jnp.float32) + theirs.astype(jnp.bfloat16).astype(
        jnp.float32
    )
    low = 0
    for n, (size, output) in enumerate(zip(sizes, outputs)):
        @pl.when((step >= low) & (step < low + size))
        def _():
            result = both
            if adds and n == 0:
                result = both + refs[chunks][0].astype(jnp.float32)
            output[0] = result.astype(jnp.bfloat16)
        low += size


def weight_terms(
    place, targets, sizes, gradient, mine, their_gradient, their_parts, arrived=(), shared=None
):
    count = len(targets)
    width, rows = gradient.shape
    half = mine.shape[2]

    def result_of(low, size):
        return pl.BlockSpec(
            (1, width, half), lambda n, place: (jnp.clip(n - low, 0, size - 1), 0, 0)
        )

    whole = pl.BlockSpec((width, rows), lambda n, place: (0, 0))
    place_of = functools.partial(block_of, targets)
    if shared is None:
        operands = [gradient, mine]
        in_specs = [whole, pl.BlockSpec((1, rows, half), place_of)]
    else:
        operands = [shared]
        in_specs = [pl.BlockSpec((1, width, half), lambda n, place: (n, 0, 0))]
    return pl.pallas_call(
        functools.partial(
            term_kernel, len(their_parts), sizes, len(arrived), shared is not None
        ),
        name="terms",
        out_shape=[jax.ShapeDtypeStruct((size, width, half), jnp.bfloat16) for size in sizes],
        grid_spec=pltpu.PrefetchScalarGridSpec(
            num_scalar_prefetch=1,
            grid=(count,),
            in_specs=[*in_specs, whole]
            + [pl.BlockSpec((1, part.shape[1], half), place_of) for part in their_parts]
            + [pl.BlockSpec((1, width, half), lambda n, place: (0, 0, 0))] * len(arrived),
            out_specs=[
                result_of(sum(sizes[:n]), size) for n, size in enumerate(sizes)
            ],
        ),
        compiler_params=pltpu.CompilerParams(vmem_limit_bytes=VMEM_LIMIT // 2),
        cost_estimate=SMALL,
    )(place, *operands, their_gradient, *their_parts, *arrived)


def total_kernel(*refs):
    output = refs[-1]
    total = refs[0][0].astype(jnp.float32)
    for block in refs[1:-1]:
        total += block[0].astype(jnp.float32)
    output[...] = total.T


def add_blocks(blocks):
    width, depth = blocks[0].shape[1:]
    return pl.pallas_call(
        total_kernel,
        name="total",
        out_shape=jax.ShapeDtypeStruct((depth, width), jnp.float32),
        grid=(1,),
        in_specs=[pl.BlockSpec((1, width, depth), lambda n: (0, 0, 0))] * len(blocks),
        out_specs=pl.BlockSpec((depth, width), lambda n: (0, 0)),
        compiler_params=pltpu.CompilerParams(vmem_limit_bytes=VMEM_LIMIT // 2),
        cost_estimate=SMALL,
    )(*blocks)


def per_device(
    queries, database, neighbor_owner, neighbor_slot, key_weight, value_weight, cotangent
):
    z, ylo, core = lax.axis_index("z"), lax.axis_index("ylo"), lax.axis_index("core")
    x, yhi = lax.axis_index("x"), lax.axis_index("yhi")
    place = jnp.stack([z, ylo, core, x, yhi]).astype(jnp.int32)
    count = neighbor_owner.shape[0] * neighbor_owner.shape[1]
    width = database.shape[2]
    owners = neighbor_owner.reshape(1, count)
    chips = owners // 2
    earlier = jnp.arange(count)[:, None] > jnp.arange(count)[None, :]
    ranks = jnp.sum((chips.reshape(count, 1) == chips) & earlier, axis=1).reshape(1, count)
    wanted = jnp.concatenate(
        [chips, owners % 2, neighbor_slot.reshape(1, count), ranks.astype(jnp.int32)], axis=1
    )
    both = jnp.concatenate([wanted, ring(wanted, "ylo", 1, 2)], axis=0)
    asked = [ring(both, "z", -n, 4) for n in (1, 2, 3)]
    across = ring(database, "core", 1, 2)

    firsts = [sum(CHUNKS[:k]) for k in range(len(CHUNKS))]

    near_hops = ((0, 0), (1, 0), (-1, 0), (0, 1), (1, 1), (-1, 1))
    far_hops = ((2, 0), (2, 1))

    def shape(k):
        return count, CHUNKS[k], width

    def hand(k, packets, *after):
        given = copies_call(
            functools.partial(collect_kernel, firsts[k], CHUNKS[k], 1), "hand", shape(k),
            [tie(place, *after), both], [database, across, packets], count,
        )
        return given, ring(given, "ylo", 1, 2)

    def merge(k, packets, given, *after):
        return copies_call(
            functools.partial(collect_kernel, firsts[k], CHUNKS[k], 0), "merge", shape(k),
            [tie(place, *after), both], [database, across, packets, given], count,
        )

    def along(values, way):
        steps = (way, -way)
        return lax.ppermute(
            values, ("core", "x"),
            [(c * 4 + i, c * 4 + (i + steps[c]) % 4) for c in range(2) for i in range(4)],
        )

    def spread_sides(own):
        own = own.reshape(-1, width)
        ahead, behind = along(own, 1), along(own, -1)
        other = ring(own, "yhi", 1, 2)
        return (own, ahead, behind, other), tie(other, ahead, behind)

    def spread(own):
        near, sent = spread_sides(own)
        return *near, along(sent, 1), along(sent, -1)

    def send_planes(packets, *after):
        return lax.all_to_all(tie(packets, *after), "z", 0, 0, tiled=True)

    packets = copies_call(
        functools.partial(pack_kernel, 0, CHUNKS[0]), "pack", (32, CHUNKS[0], width),
        [place, both, *asked], [database, across], 8 * count,
    )
    arrived = lax.all_to_all(packets, ("z", "ylo"), 0, 0, tiled=True)
    planes = [packets]
    for k in range(1, len(CHUNKS)):
        planes.append(
            copies_call(
                functools.partial(planes_kernel, firsts[k], CHUNKS[k]), "planes",
                (32, CHUNKS[k], width), [tie(place, planes[-1]), *asked], [database, across],
                6 * count,
            )
        )
    own = copies_call(merge_kernel, "merge", shape(0), [tie(wanted, planes[-1])], [arrived], count)
    by_plane = send_planes(planes[1], own)
    near = spread(own)
    far = (along(near[1], 1),)
    handed, given = hand(1, by_plane, *near[1:4])
    far += (along(tie(near[5], handed), -1),)
    own = merge(1, by_plane, given, *near[4:], far[0])
    matrices = (key_weight, value_weight)
    keys, mine, theirs, values = project(
        tie(place, own), (*near, *far), near_hops + far_hops, 0, matrices
    )
    near, other = spread_sides(own)
    far = along(tie(near[1], keys), 1)
    steps = [(near, near_hops[:4]), ((far,), far_hops[:1])]
    begun, last_theirs = None, None
    for n in range(3):
        if n == 1:
            sent = tie(other, far, key_sum)
            steps.append((
                (along(sent, 1), along(sent, -1), ring(far, "yhi", 1, 2)),
                near_hops[4:] + far_hops[1:],
            ))
        pieces, hops = steps[n]
        key_sum, mine, last_theirs, value_sum = project(
            place, pieces, hops, firsts[1] * count, matrices, mine, last_theirs, begun, n == 2
        )
        begun = key_sum, value_sum
    key_parts, value_parts = [keys, key_sum], [values, value_sum]
    their_parts = [ring(theirs, "core", 1, 2), ring(last_theirs, "core", 1, 2)]

    chances, gradient = weigh(queries, cotangent, key_parts)
    their_gradient = ring(gradient, "core", 1, 2)
    def terms(targets, sizes, arrived=(), after=(), shared=None):
        return weight_terms(
            tie(place, *after), targets, sizes, gradient, mine, their_gradient, their_parts,
            arrived, shared,
        )

    planes_of = (1, 0), (1, 1), (3, 0), (3, 1)
    shared = own_terms(place, planes_of, gradient, mine)
    ahead, behind = terms(planes_of, (2, 2), shared=shared)
    corner, = terms(((2, 1),), (1,), (), (behind,))
    beside, here = terms(((0, 1), (0, 0)), (1, 1), (), (corner,))
    far, = terms(((2, 0),), (1,), (ring(corner, "ylo", 1, 2),), (here,))
    beside = tie(beside, far)
    ahead, behind = ring(ahead, "z", 1, 4), ring(behind, "z", -1, 4)
    far = ring(far, "z", 2, 4)
    beside = beside.astype(jnp.float32) + ahead[1:] + behind[1:]
    beside = ring(beside.astype(jnp.bfloat16), "ylo", 1, 2)
    attended, query_grad = attend(cotangent, chances, key_parts, value_parts)
    value_weight_grad = add_blocks(
        [ahead, behind, far, here, tie(beside, attended)]
    )
    return attended, query_grad, value_weight_grad


def solution(mesh):
    inner = Mesh(mesh.devices.reshape(4, 2, 2, 4, 2), (*DB, *MP))
    return jax.shard_map(
        per_device,
        mesh=inner,
        in_specs=(
            P(DB, MP),
            P(DB, None, MP),
            P(DB, None),
            P(DB, None),
            P(None, MP),
            P(None, MP),
            P(DB, MP),
        ),
        out_specs=(P(DB, MP), P(DB, MP), P(DB, MP)),
        check_vma=False,
    )
```
